32 devices in a mesh: grp: 2 (over x), det: 16 (over z, y, core).
Axes of the slice: x: 2, y: 2, z: 4, core: 2. Of those that a mesh axis runs over, the one named last changes fastest.
Arguments:
- timestream: float32 [2, 1024, 16384], P('grp', 'det'), parts along dimension 0, may hold values from -6 to 6
- gains: float32 [2, 1024], P('grp', 'det'), parts along dimension 0, may hold values from 0.5 to 2
- mode_pattern: float32 [2048, 256], P('grp'), parts along dimension 0, may hold values from -0.375 to 0.375
- mode_weights: float32 [2048, 256], P('grp'), parts along dimension 0, may hold values from -0.1875 to 0.1875
- noise_weight: float32 [2048, 16384], P(('grp', 'det')), parts along dimension 0, may hold values from 0.05 to 1
- block_ids: int32 [2, 1024, 64], P('grp', 'det'), parts along dimension 0, may hold values from 0 to 255
- hits: int32 [2, 1024, 64], P('grp', 'det'), parts along dimension 0, may hold values from 0 to 3
- sky_rows: int32 [512], P('grp'), parts along dimension 0, may hold values from 0 to 255, each once
Outputs:
- filtered: float32 [2, 1024, 16384], P('grp', 'det'), parts along dimension 0
- sky_map: float32 [512, 256], P(('grp', 'det')), parts along dimension 0
The draws below stay inside these ranges and needn't reach their ends.
There are 2 independent parts, one for each index of `grp`. The reference program is written for one: setup_inputs(seed, part) draws one part's arguments, and reference() takes and returns one part's arrays. A program takes and returns all parts, laid end to end along the dimension named above; each array names one. Nothing has to cross between parts.
Inputs may be any that keep to these rules, and one draw needn't show every extreme that they name: `sky_rows`: each row number appears exactly once.
All inputs are finite; a program needn't handle non-finite values.
Results may differ from the reference program's by a relative error of at most 0.000078.
Values sent between devices are 32-bit elements; how exact they have to be, the bound alone decides.
A program may use at most 128 MiB of HBM per device.

```python
import math
import jax
import jax.numpy as jnp
import numpy as np
from jax import lax

ND = 1024
NS = 16384
RANK = 256
PIX = 256
OBS = 1
NB = 256
NT = 64


def touch_ends(result, own_key, smallest, largest):
    extent = result.shape
    spot = [jax.random.randint(jax.random.fold_in(own_key, axis), (), 0, extent[axis]) for axis in range(len(extent))]
    result = result.at[tuple(spot)].set(smallest)
    longest = extent.index(max(extent))
    spot[longest] = (spot[longest] + 1) % extent[longest]
    return result.at[tuple(spot)].set(largest)


def block_levels(own_key, dims, pieces, low, top_value):
    gain = 1.0
    for axis_at, blocks in pieces:
        draws = jax.random.uniform(jax.random.fold_in(jax.random.fold_in(own_key, 6), axis_at), (blocks,), jnp.float32, low / len(pieces), top_value / len(pieces))
        gain = gain * jnp.repeat(jnp.exp(draws), dims[axis_at] // blocks).reshape((-1,) + (1,) * (len(dims) - 1 - axis_at))
    return gain


def rank_table(number_of, lean):
    loads = [(1 << 20) // math.isqrt(standing ** lean) + 1 for standing in range(1, number_of + 1)]
    deviation = 1 + sum(loads) // (1 << 30)
    return np.cumsum(np.array([max(1, weight // deviation) for weight in loads]))


def skewed_ids(stream_key, extent, count, lean):
    grid = rank_table(count, lean)
    pick = jax.random.randint(jax.random.fold_in(stream_key, 1), extent, 0, int(grid[count - 1]))
    grade = jnp.searchsorted(jnp.asarray(grid, jnp.int32), pick, side="right")
    return jax.random.permutation(jax.random.fold_in(stream_key, 2), count)[grade].astype(jnp.int32)


def gaussian(stream_key, dims, spread, reach, shards=(), held_as=jnp.bfloat16):
    result = spread * jax.random.normal(stream_key, dims, jnp.float32)
    if shards:
        result = result * block_levels(stream_key, dims, shards, -0.22, 0.18)
    return jnp.clip(result, -reach, reach).astype(held_as)


def setup_inputs(seed: int = 0, part: int = 0) -> dict:
    key_list = jax.random.split(jax.random.key(seed), 9)
    part_keys = jax.random.split(jax.random.fold_in(key_list[8], part), 9)
    timestream = gaussian(part_keys[0], (OBS, ND, NS), 1.0, 6.0, ((1, 16),), jnp.float32)
    gains = jnp.clip(jnp.exp(math.log(2.0) - 1.3862944 * jax.random.uniform(part_keys[1], (OBS, ND), jnp.float32) ** block_levels(part_keys[1], (OBS, ND), ((1, 16),), -0.2, 0.2)), 0.5, 2.0)
    mode_pattern = gaussian(part_keys[2], (ND, RANK), RANK ** -0.5, 0.375, (), jnp.float32)
    mode_weights = gaussian(part_keys[3], (ND, RANK), ND ** -0.5, 0.1875, (), jnp.float32)
    noise_weight = jnp.clip(jnp.exp(math.log(1.0) - 2.9957323 * jax.random.uniform(part_keys[4], (ND, NS), jnp.float32) ** block_levels(part_keys[4], (ND, NS), ((0, 16),), -0.2, 0.2)), 0.05, 1.0)
    block_ids = touch_ends(skewed_ids(part_keys[5], (OBS, ND, NT), NB, 2), jax.random.fold_in(part_keys[5], 3), 0, NB - 1).astype(jnp.int32)
    hits = touch_ends(jax.random.randint(part_keys[6], (OBS, ND, NT), 0, 4), jax.random.fold_in(part_keys[6], 1), 0, 3).astype(jnp.int32)
    sky_rows = jax.random.permutation(part_keys[7], NB).astype(jnp.int32)
    return {"timestream": timestream, "gains": gains, "mode_pattern": mode_pattern, "mode_weights": mode_weights, "noise_weight": noise_weight, "block_ids": block_ids, "hits": hits, "sky_rows": sky_rows}


def reference(timestream, gains, mode_pattern, mode_weights, noise_weight, block_ids, hits, sky_rows):
    highest = lax.Precision.HIGHEST
    calibrated = timestream / gains[:, :, None]

    def one_observation(signal):
        coeff = jnp.dot(mode_weights.T, signal, precision=highest, preferred_element_type=jnp.float32)
        corrected = signal - jnp.dot(mode_pattern, coeff, precision=highest, preferred_element_type=jnp.float32)
        spectrum = jnp.fft.fft(corrected, axis=1)
        return jnp.real(jnp.fft.ifft(spectrum * noise_weight, axis=1)).astype(jnp.float32)
    filtered = lax.map(one_observation, calibrated)
    tiles = filtered.reshape(OBS * ND * NT, PIX)
    weight = hits.reshape(-1).astype(jnp.float32)
    rows = sky_rows[block_ids.reshape(-1)]
    sums = jax.ops.segment_sum(tiles * weight[:, None], rows, num_segments=NB)
    counts = jax.ops.segment_sum(weight, rows, num_segments=NB)
    sky_map = sums / jnp.sqrt(1.0 + counts)[:, None]
    return (filtered, sky_map)
```

```python
import functools
import math

import jax
import jax.numpy as jnp
import ml_dtypes
import numpy as np
from jax import lax
from jax.experimental import pallas as pl
from jax.experimental.pallas import tpu as pltpu
from jax.sharding import PartitionSpec as P

PIX = 256
LANES = 128
MIB = 1 << 20


def split(value):
    high = value.astype(jnp.bfloat16)
    return high, (value - high.astype(jnp.float32)).astype(jnp.bfloat16)


def product(left, right):
    dot = functools.partial(jnp.dot, preferred_element_type=jnp.float32)
    return dot(left[0], right[0]) + (dot(left[0], right[1]) + dot(left[1], right[0]))


def halves(table):
    high = table.astype(ml_dtypes.bfloat16)
    low = (table - high.astype(np.float64)).astype(ml_dtypes.bfloat16)
    return np.stack([high, low])


def transform_tables(side):
    index = np.arange(side)
    angle = (np.outer(index, index) % side) * (2.0 * math.pi / side)
    cos, sin = np.cos(angle), np.sin(angle)
    twist = np.outer(index, index) * (2.0 * math.pi / (side * side))
    turn = np.stack([np.cos(twist), np.sin(twist)]).astype(np.float32)
    last = np.concatenate([cos, -sin], 1) / (side * side)
    per_row = PIX // side
    last = last.reshape(side // per_row, per_row, 2 * side).swapaxes(0, 1).reshape(side, 2 * side)
    return (
        halves(np.concatenate([cos, -sin], 0)),
        halves(np.block([[cos, -sin], [sin, cos]])),
        halves(np.block([[cos, sin], [-sin, cos]])),
        halves(last),
        turn,
    )


def correct_kernel(
    plane, planes, chunks, x_ref, gain_ref, weight_ref, pattern_ref, out_ref,
    cal, slab, part, to_right, to_left, from_left, from_right, back,
    raw_send, raw_recv, right_send, right_recv, left_send, left_recv, back_send, back_recv,
):
    me = lax.axis_index("det")
    z, q = me // plane, me % plane
    dets, samples = x_ref.shape
    quarter = samples // plane
    width = quarter // chunks
    first, last = z == 0, z == planes - 1

    barrier = pltpu.get_barrier_semaphore()

    def partner(step):
        return lax.rem(q + step, plane)

    for step in range(1, plane):
        pl.semaphore_signal(barrier, inc=1, device_id={"det": z * plane + partner(step)})

    @pl.when(z > 0)
    def _():
        pl.semaphore_signal(barrier, inc=1, device_id={"det": me - plane})

    @pl.when(z < planes - 1)
    def _():
        pl.semaphore_signal(barrier, inc=1, device_id={"det": me + plane})

    at_ends = (z == 0).astype(jnp.int32) + (z == planes - 1).astype(jnp.int32)
    pl.semaphore_wait(barrier, plane + 1 - at_ends)

    def span(owner, chunk):
        return pl.ds(pl.multiple_of(owner * quarter + chunk * width, width), width)

    def raw_copy(chunk, step):
        other = partner(step)
        return pltpu.make_async_remote_copy(
            src_ref=cal.at[:, span(other, chunk)],
            dst_ref=slab.at[chunk, pl.ds(pl.multiple_of(q * dets, 8), dets), :],
            send_sem=raw_send.at[chunk, step - 1],
            recv_sem=raw_recv.at[chunk, step - 1],
            device_id={"det": z * plane + other},
        )

    def back_copy(chunk, step):
        other = partner(step)
        return pltpu.make_async_remote_copy(
            src_ref=back.at[chunk, pl.ds(pl.multiple_of(other * dets, 8), dets), :],
            dst_ref=out_ref.at[:, span(q, chunk)],
            send_sem=back_send.at[chunk, step - 1],
            recv_sem=back_recv.at[chunk, step - 1],
            device_id={"det": z * plane + other},
        )

    def right_copy(chunk):
        return pltpu.make_async_remote_copy(
            src_ref=to_right.at[chunk],
            dst_ref=from_left.at[chunk],
            send_sem=right_send.at[chunk],
            recv_sem=right_recv.at[chunk],
            device_id={"det": lax.rem(me + plane, plane * planes)},
        )

    def left_copy(chunk):
        return pltpu.make_async_remote_copy(
            src_ref=to_left.at[chunk],
            dst_ref=from_right.at[chunk],
            send_sem=left_send.at[chunk],
            recv_sem=left_recv.at[chunk],
            device_id={"det": lax.rem(me + plane * (planes - 1), plane * planes)},
        )

    own_rows = pl.ds(pl.multiple_of(q * dets, 8), dets)

    def send_raw(chunk, carry):
        for owner in range(plane):
            cal[:, span(owner, chunk)] = x_ref[:, span(owner, chunk)] / gain_ref[...]
        for step in range(1, plane):
            raw_copy(chunk, step).start()
        slab[chunk, own_rows, :] = cal[:, span(q, chunk)]
        return carry

    lax.fori_loop(0, chunks, send_raw, 0)

    weight = split(weight_ref[...])
    pattern = split(pattern_ref[...])

    def one_step(i, carry):
        @pl.when(i < chunks)
        def _():
            for step in range(1, plane):
                raw_copy(i, step).wait_recv()
            part[i] = product(weight, split(slab[i]))

        c_right = i - z

        @pl.when((c_right >= 0) & (c_right < chunks))
        def _():
            @pl.when(first)
            def _():
                from_left[c_right] = jnp.zeros(part.shape[1:], jnp.float32)
                to_right[c_right] = part[c_right]

            @pl.when(z > 0)
            def _():
                right_copy(c_right).wait_recv()
                to_right[c_right] = part[c_right] + from_left[c_right]

            @pl.when(z < planes - 1)
            def _():
                right_copy(c_right).start()

        c_left = i - (planes - 1 - z)

        @pl.when((c_left >= 0) & (c_left < chunks))
        def _():
            @pl.when(last)
            def _():
                from_right[c_left] = jnp.zeros(part.shape[1:], jnp.float32)
                to_left[c_left] = part[c_left]

            @pl.when(z < planes - 1)
            def _():
                left_copy(c_left).wait_recv()
                to_left[c_left] = part[c_left] + from_right[c_left]

            @pl.when(z > 0)
            def _():
                left_copy(c_left).start()

        c = i - (planes - 1)

        @pl.when(c >= 0)
        def _():
            coeff = to_right[c] + from_right[c]
            back[c] = slab[c] - product(pattern, split(coeff))
            for step in range(1, plane):
                back_copy(c, step).start()
            out_ref[:, span(q, c)] = back[c, own_rows, :]

        return carry

    lax.fori_loop(0, chunks + planes - 1, one_step, 0)

    def finish(chunk, carry):
        for step in range(1, plane):
            back_copy(chunk, step).wait_recv()
            back_copy(chunk, step).wait_send()
            raw_copy(chunk, step).wait_send()

        @pl.when(z < planes - 1)
        def _():
            right_copy(chunk).wait_send()

        @pl.when(z > 0)
        def _():
            left_copy(chunk).wait_send()

        return carry

    lax.fori_loop(0, chunks, finish, 0)


def correct(stream, gains, mode_pattern, mode_weights, size):
    dets, samples = stream.shape
    rank = mode_pattern.shape[1]
    plane = 4 if size % 4 == 0 else 1
    planes = size // plane
    quarter = samples // plane
    chunks = max(1, quarter // 256)
    width = quarter // chunks
    rows = plane * dets
    start = (lax.axis_index("det") // plane) * rows
    weights = lax.dynamic_slice_in_dim(mode_weights, start, rows, 0).T
    pattern = lax.dynamic_slice_in_dim(mode_pattern, start, rows, 0)
    f32 = jnp.float32
    sem = pltpu.SemaphoreType.DMA
    coeffs = pltpu.VMEM((chunks, rank, width), f32)
    block = pltpu.VMEM((chunks, rows, width), f32)
    return pl.pallas_call(
        functools.partial(correct_kernel, plane, planes, chunks),
        out_shape=jax.ShapeDtypeStruct((dets, samples), f32),
        in_specs=[pl.BlockSpec(memory_space=pltpu.VMEM)] * 4,
        out_specs=pl.BlockSpec(memory_space=pltpu.VMEM),
        scratch_shapes=[
            pltpu.VMEM((dets, samples), f32), block, coeffs, coeffs, coeffs, coeffs, coeffs, block,
            sem((chunks, plane)), sem((chunks, plane)), sem((chunks,)), sem((chunks,)),
            sem((chunks,)), sem((chunks,)), sem((chunks, plane)), sem((chunks, plane)),
        ],
        compiler_params=pltpu.CompilerParams(
            collective_id=0, has_side_effects=True, vmem_limit_bytes=56 * MIB
        ),
        name="correct",
    )(stream, gains.reshape(dets, 1), weights, pattern)


def filter_kernel(x_ref, w_ref, row_ref, hit_ref, t1, t2, t3, t4, turn, out_ref, acc_ref):
    batch, side, _ = x_ref.shape
    per_row = PIX // side
    tiles = side // per_row
    cos, sin = turn[0], turn[1]
    signal = jnp.concatenate([x_ref[b] for b in range(batch)], axis=1)
    section = product((t1[0], t1[1]), split(signal))
    turned = []
    for b in range(batch):
        real, imag = section[:side, b * side:(b + 1) * side], section[side:, b * side:(b + 1) * side]
        turned.append(jnp.concatenate([real * cos + imag * sin, imag * cos - real * sin], axis=1))
    freq = product(split(jnp.concatenate(turned, axis=0)), (t2[0], t2[1]))
    weighted = []
    for b in range(batch):
        weight = w_ref[b].T
        weighted.append(freq[b * side:(b + 1) * side] * jnp.concatenate([weight, weight], axis=1))
    section = product(split(jnp.concatenate(weighted, axis=0)), (t3[0], t3[1]))
    turned = []
    for b in range(batch):
        real, imag = section[b * side:(b + 1) * side, :side], section[b * side:(b + 1) * side, side:]
        turned.append(jnp.concatenate([real * cos - imag * sin, imag * cos + real * sin], axis=0))
    result = product((t4[0], t4[1]), split(jnp.concatenate(turned, axis=1)))
    tiled = []
    for b in range(batch):
        column = result[:, b * side:(b + 1) * side]
        tiled.append(jnp.concatenate([column[p * tiles:(p + 1) * tiles] for p in range(per_row)], axis=1))
        out_ref[b] = tiled[b]
    high, low = split(jnp.concatenate(tiled, axis=0))
    blocks = acc_ref.shape[0]
    ladder = lax.broadcasted_iota(jnp.int32, (blocks, batch * tiles), 0)
    table = jnp.where(row_ref[...] == ladder, hit_ref[...], 0.0)
    half = table.astype(jnp.bfloat16)
    dot = functools.partial(jnp.dot, preferred_element_type=jnp.float32)
    sums = dot(half, high) + dot(half, low)
    counts = table[:, :LANES]
    for at in range(LANES, batch * tiles, LANES):
        counts = counts + table[:, at:at + LANES]

    @pl.when(pl.program_id(0) == 0)
    def _():
        acc_ref[...] = jnp.zeros_like(acc_ref)

    acc_ref[:, :PIX] += sums
    acc_ref[:, PIX:] += counts


def filter_and_bin(signal, weight, rows, hits, blocks):
    dets, side, _ = signal.shape
    tables = transform_tables(side)
    batch = 4
    tiles = side * side // PIX
    whole = lambda table: pl.BlockSpec(table.shape, lambda i: (0,) * table.ndim)
    cube = pl.BlockSpec((batch, side, side), lambda i: (i, 0, 0))
    line = pl.BlockSpec((1, batch * tiles), lambda i: (0, i))
    return pl.pallas_call(
        filter_kernel,
        grid=(dets // batch,),
        out_shape=(
            jax.ShapeDtypeStruct((dets, tiles, PIX), jnp.float32),
            jax.ShapeDtypeStruct((blocks, PIX + LANES), jnp.float32),
        ),
        in_specs=[cube, cube, line, line] + [whole(table) for table in tables],
        out_specs=(
            pl.BlockSpec((batch, tiles, PIX), lambda i: (i, 0, 0)),
            pl.BlockSpec((blocks, PIX + LANES), lambda i: (0, 0)),
        ),
        compiler_params=pltpu.CompilerParams(vmem_limit_bytes=48 * MIB),
        name="filter_bin",
    )(signal, weight, rows, hits, *[jnp.asarray(table) for table in tables])


def map_kernel(size, acc_ref, out_ref, landed, send_sem, recv_sem):
    me = lax.axis_index("det")
    rows = out_ref.shape[0]
    barrier = pltpu.get_barrier_semaphore()

    def greet(step, carry):
        pl.semaphore_signal(barrier, inc=1, device_id={"det": lax.rem(me + step, size)})
        return carry

    lax.fori_loop(1, size, greet, 0)
    pl.semaphore_wait(barrier, size - 1)

    def copy(step):
        other = lax.rem(me + step, size)
        return pltpu.make_async_remote_copy(
            src_ref=acc_ref.at[pl.ds(pl.multiple_of(other * rows, 8), rows), :],
            dst_ref=landed.at[step],
            send_sem=send_sem.at[step],
            recv_sem=recv_sem.at[step],
            device_id={"det": other},
        )

    def start(step, carry):
        copy(step).start()
        return carry

    lax.fori_loop(1, size, start, 0)

    def add(step, total):
        copy(step).wait_recv()
        return total + landed[step]

    own = acc_ref[pl.ds(pl.multiple_of(me * rows, 8), rows), :]
    total = lax.fori_loop(1, size, add, own)
    counts = jnp.sum(total[:, PIX:], axis=1, keepdims=True)
    out_ref[...] = total[:, :PIX] / jnp.sqrt(1.0 + counts)

    def finish(step, carry):
        copy(step).wait_send()
        return carry

    lax.fori_loop(1, size, finish, 0)


def combine_map(acc, size):
    blocks, columns = acc.shape
    rows = blocks // size
    return pl.pallas_call(
        functools.partial(map_kernel, size),
        out_shape=jax.ShapeDtypeStruct((rows, PIX), jnp.float32),
        in_specs=[pl.BlockSpec(memory_space=pltpu.VMEM)],
        out_specs=pl.BlockSpec(memory_space=pltpu.VMEM),
        scratch_shapes=[
            pltpu.VMEM((size, rows, columns), jnp.float32),
            pltpu.SemaphoreType.DMA((size,)),
            pltpu.SemaphoreType.DMA((size,)),
        ],
        compiler_params=pltpu.CompilerParams(collective_id=1, has_side_effects=True),
        name="combine_map",
    )(acc)


def shards(size, timestream, gains, mode_pattern, mode_weights, noise_weight, block_ids, hits, sky_rows):
    items, dets, samples = timestream.shape
    side = math.isqrt(samples)
    ids_flat = block_ids.reshape(-1)
    blocks = sky_rows.shape[0]
    ladder = lax.broadcasted_iota(jnp.int32, (blocks, ids_flat.shape[0]), 0)
    rows = jnp.sum(jnp.where(ids_flat[None, :] == ladder, sky_rows[:, None], 0), axis=0)
    weight = hits.reshape(1, -1).astype(jnp.float32)
    corrected = correct(timestream.reshape(items * dets, samples), gains.reshape(-1), mode_pattern, mode_weights, size)
    filtered, acc = filter_and_bin(
        corrected.reshape(dets, side, side), noise_weight.reshape(dets, side, side), rows[None, :], weight, blocks
    )
    return (filtered.reshape(items, dets, samples), combine_map(acc, size))


def solution(mesh):
    in_specs = (
        P("grp", "det", None),
        P("grp", "det"),
        P("grp", None),
        P("grp", None),
        P(("grp", "det"), None),
        P("grp", "det", None),
        P("grp", "det", None),
        P("grp"),
    )
    out_specs = (P("grp", "det", None), P(("grp", "det"), None))
    body = functools.partial(shards, mesh.shape["det"])
    return jax.shard_map(body, mesh=mesh, in_specs=in_specs, out_specs=out_specs, check_vma=False)
```

```python
import functools
import math

import jax
import jax.numpy as jnp
import ml_dtypes
import numpy as np
from jax import lax
from jax.experimental import pallas as pl
from jax.experimental.pallas import tpu as pltpu
from jax.sharding import PartitionSpec as P

PIX = 256
LANES = 128
MIB = 1 << 20


def split(value):
    high = value.astype(jnp.bfloat16)
    return high, (value - high.astype(jnp.float32)).astype(jnp.bfloat16)


def product(left, right):
    dot = functools.partial(jnp.dot, preferred_element_type=jnp.float32)
    return dot(left[0], right[0]) + (dot(left[0], right[1]) + dot(left[1], right[0]))


def halves(table):
    high = table.astype(ml_dtypes.bfloat16)
    low = (table - high.astype(np.float64)).astype(ml_dtypes.bfloat16)
    return np.stack([high, low])


def transform_tables(side):
    index = np.arange(side)
    angle = (np.outer(index, index) % side) * (2.0 * math.pi / side)
    cos, sin = np.cos(angle), np.sin(angle)
    packed = np.stack([cos[: side // 2], -sin[: side // 2]], 1).reshape(side, side)
    packed[1] = cos[side // 2]
    twist = np.outer(np.arange(side // 2 + 1), index) * (2.0 * math.pi / (side * side))
    turn = np.stack([np.cos(twist), np.sin(twist)]).astype(np.float32)
    per_row = PIX // side
    last = packed.T / (side * side)
    last = last.reshape(side // per_row, per_row, side).swapaxes(0, 1).reshape(side, side)
    return (
        halves(packed),
        halves(np.block([[cos, -sin], [sin, cos]])),
        halves(np.block([[cos, sin], [-sin, cos]])),
        np.eye(side)[::-1].astype(ml_dtypes.bfloat16),
        turn,
        halves(last),
    )


def correct_kernel(
    plane, planes, x_ref, gain_ref, noise_ref, weight_ref, pattern_ref, t1, t2, t3, flip, turn, out_ref,
    cube, cal, slab, part, from_left, from_right, land, fold,
    raw_send, raw_recv, right_send, right_recv, left_send, left_recv, back_send, back_recv,
):
    me = lax.axis_index("det")
    z, q = me // plane, me % plane
    dets, samples = x_ref.shape
    side = t1.shape[1]
    chunks = side // plane
    hop = 2
    lag = hop * (planes - 1)
    mid_lag = max(lag + 2, 8)

    barrier = pltpu.get_barrier_semaphore()

    def partner(step):
        return lax.rem(q + step, plane)

    for step in range(1, plane):
        pl.semaphore_signal(barrier, inc=1, device_id={"det": z * plane + partner(step)})

    @pl.when(z > 0)
    def _():
        pl.semaphore_signal(barrier, inc=1, device_id={"det": me - plane})

    @pl.when(z < planes - 1)
    def _():
        pl.semaphore_signal(barrier, inc=1, device_id={"det": me + plane})

    def column(row):
        return pl.ds(pl.multiple_of(row * side, side), side)

    def spread(row):
        return pl.ds(row, dets, stride=side)

    def own_rows(owner):
        return pl.ds(pl.multiple_of(owner * dets, 8), dets)

    def raw_copy(chunk, step):
        other = partner(step)
        return pltpu.make_async_remote_copy(
            src_ref=cal.at[:, column(other * chunks + chunk)],
            dst_ref=slab.at[chunk, own_rows(q), :],
            send_sem=raw_send.at[chunk, step - 1],
            recv_sem=raw_recv.at[chunk, step - 1],
            device_id={"det": z * plane + other},
        )

    def back_copy(chunk, step):
        other = partner(step)
        return pltpu.make_async_remote_copy(
            src_ref=slab.at[chunk, own_rows(other), :],
            dst_ref=land.at[:, column(q * chunks + chunk)],
            send_sem=back_send.at[chunk, step - 1],
            recv_sem=back_recv.at[chunk, step - 1],
            device_id={"det": z * plane + other},
        )

    def right_copy(chunk):
        return pltpu.make_async_remote_copy(
            src_ref=from_left.at[chunk, 1],
            dst_ref=from_left.at[chunk, 0],
            send_sem=right_send.at[chunk],
            recv_sem=right_recv.at[chunk],
            device_id={"det": lax.rem(me + plane, plane * planes)},
        )

    def left_copy(chunk):
        return pltpu.make_async_remote_copy(
            src_ref=from_right.at[chunk, 1],
            dst_ref=from_right.at[chunk, 0],
            send_sem=left_send.at[chunk],
            recv_sem=left_recv.at[chunk],
            device_id={"det": lax.rem(me + plane * (planes - 1), plane * planes)},
        )

    gain = gain_ref[...]

    def to_cube(row, carry):
        cube[spread(row), :] = x_ref[:, column(row)] / gain
        return carry

    lax.fori_loop(0, side, to_cube, 0, unroll=4)
    first_table = (t1[0], t1[1])
    group = 8

    def first_stage(at, carry):
        rows = [pl.ds(pl.multiple_of((at * group + d) * side, side), side) for d in range(group)]
        section = product(first_table, split(jnp.concatenate([cube[row, :] for row in rows], axis=1)))
        for d in range(group):
            cube[rows[d], :] = section[:, d * side:(d + 1) * side]
        return carry

    lax.fori_loop(0, dets // group, first_stage, 0)
    at_ends = (z == 0).astype(jnp.int32) + (z == planes - 1).astype(jnp.int32)
    pl.semaphore_wait(barrier, plane + 1 - at_ends)

    def send_raw(chunk, carry):
        for owner in range(plane):
            row = owner * chunks + chunk
            cal[:, column(row)] = cube[spread(row), :]
        for step in range(1, plane):
            raw_copy(chunk, step).start()
        slab[chunk, own_rows(q), :] = cal[:, column(q * chunks + chunk)]
        return carry

    lax.fori_loop(0, chunks, send_raw, 0)
    weight = split(weight_ref[...])
    pattern = split(pattern_ref[...])

    def middle(real, imag, slots):
        turned = []
        for r, m, k in zip(real, imag, slots):
            cos, sin = turn[0, pl.ds(k, 1), :], turn[1, pl.ds(k, 1), :]
            turned.append(jnp.concatenate([r * cos + m * sin, m * cos - r * sin], axis=1))
        freq = product(split(jnp.concatenate(turned, axis=0)), (t2[0], t2[1]))
        weighted = []
        for at, k in enumerate(slots):
            noise = fold[own_rows(k), :]
            weighted.append(freq[at * dets:(at + 1) * dets] * jnp.concatenate([noise, noise], axis=1))
        section = product(split(jnp.concatenate(weighted, axis=0)), (t3[0], t3[1]))
        result = []
        for at, k in enumerate(slots):
            cos, sin = turn[0, pl.ds(k, 1), :], turn[1, pl.ds(k, 1), :]
            r, m = section[at * dets:(at + 1) * dets, :side], section[at * dets:(at + 1) * dets, side:]
            result.append((r * cos - m * sin, m * cos + r * sin))
        return result

    def one_step(i, carry):
        @pl.when(i < chunks)
        def _():
            for step in range(1, plane):
                raw_copy(i, step).wait_recv()
            part[i] = product(weight, split(slab[i]))

        c_right = i - hop * z

        @pl.when((c_right >= 0) & (c_right < chunks))
        def _():
            @pl.when(z == 0)
            def _():
                from_left[c_right, 1] = part[c_right]

            @pl.when(z > 0)
            def _():
                right_copy(c_right).wait_recv()
                from_left[c_right, 1] = part[c_right] + from_left[c_right, 0]

            @pl.when(z < planes - 1)
            def _():
                right_copy(c_right).start()

        c_left = i - hop * (planes - 1 - z)

        @pl.when((c_left >= 0) & (c_left < chunks))
        def _():
            @pl.when(z == planes - 1)
            def _():
                from_right[c_left, 1] = part[c_left]

            @pl.when(z < planes - 1)
            def _():
                left_copy(c_left).wait_recv()
                from_right[c_left, 1] = part[c_left] + from_right[c_left, 0]

            @pl.when(z > 0)
            def _():
                left_copy(c_left).start()

        c = i - lag

        @pl.when((c >= 0) & (c < chunks))
        def _():
            coeff = from_left[c, 1] + (from_right[c, 1] - part[c])
            slab[c] = slab[c] - product(pattern, split(coeff))
            for step in range(1, plane):
                back_copy(c, step).start()
            land[:, column(q * chunks + c)] = slab[c, own_rows(q), :]

        @pl.when(i < 4)
        def _():
            def regroup(at, carry):
                row = i * (side // 4) + at
                cube[spread(row), :] = noise_ref[:, column(row)]
                return carry

            lax.fori_loop(0, side // 4, regroup, 0, unroll=4)

        @pl.when((i >= 4) & (i < 8))
        def _():
            def swap(at, carry):
                det = (i - 4) * (dets // 4) + at
                fold[pl.ds(det, side, stride=dets), :] = cube[column(det), :].T
                return carry

            lax.fori_loop(0, dets // 4, swap, 0)

        @pl.when(i == 8)
        def _():
            def add_mirror(k, carry):
                high, low = split(fold[own_rows(side - k), :])
                dot = functools.partial(jnp.dot, preferred_element_type=jnp.float32)
                fold[own_rows(k), :] += dot(high, flip[...]) + dot(low, flip[...])
                return carry

            lax.fori_loop(1, side // 2, add_mirror, 0)

        pair = (i - mid_lag - 1) // 2

        @pl.when((i > mid_lag) & ((i - mid_lag) % 2 == 1) & (pair < chunks // 2))
        def _():
            for step in range(1, plane):
                back_copy(2 * pair, step).wait_recv()
                back_copy(2 * pair + 1, step).wait_recv()
            slots = [owner * (chunks // 2) + pair for owner in range(plane)]
            real = [land[:, column(2 * k)] for k in slots]
            imag = [land[:, column(2 * k + 1)] for k in slots]
            for k, (r, m) in zip(slots, middle(real, imag, slots)):
                out_ref[spread(2 * k), :] = r
                out_ref[spread(2 * k + 1), :] = m

            @pl.when(pair == 0)
            def _():
                none = jnp.zeros((dets, side), jnp.float32)
                ends = middle([real[0], imag[0]], [none, none], [0, side // 2])
                out_ref[spread(0), :] = ends[0][0]
                out_ref[spread(1), :] = ends[1][0]

        return carry

    lax.fori_loop(0, chunks + mid_lag + 1, one_step, 0)

    def finish(chunk, carry):
        for step in range(1, plane):
            back_copy(chunk, step).wait_send()
            raw_copy(chunk, step).wait_send()

        @pl.when(z < planes - 1)
        def _():
            right_copy(chunk).wait_send()

        @pl.when(z > 0)
        def _():
            left_copy(chunk).wait_send()

        return carry

    lax.fori_loop(0, chunks, finish, 0)


def correct(stream, gains, noise, mode_pattern, mode_weights, tables, size):
    dets, samples = stream.shape
    rank = mode_pattern.shape[1]
    side = math.isqrt(samples)
    plane = 4 if size % 4 == 0 else 1
    planes = size // plane
    chunks = side // plane
    rows = plane * dets
    start = (lax.axis_index("det") // plane) * rows
    weights = lax.dynamic_slice_in_dim(mode_weights, start, rows, 0).T
    pattern = lax.dynamic_slice_in_dim(mode_pattern, start, rows, 0)
    f32 = jnp.float32
    sem = pltpu.SemaphoreType.DMA
    coeffs = pltpu.VMEM((chunks, rank, side), f32)
    chain = pltpu.VMEM((chunks, 2, rank, side), f32)
    whole = pltpu.VMEM((dets, samples), f32)
    cube = pltpu.VMEM((dets * side, side), f32)
    return pl.pallas_call(
        functools.partial(correct_kernel, plane, planes),
        out_shape=jax.ShapeDtypeStruct((dets * side, side), f32),
        in_specs=[pl.BlockSpec(memory_space=pltpu.VMEM)] * (5 + len(tables)),
        out_specs=pl.BlockSpec(memory_space=pltpu.VMEM),
        scratch_shapes=[
            cube, whole, pltpu.VMEM((chunks, rows, side), f32), coeffs, chain, chain, whole, cube,
            sem((chunks, plane)), sem((chunks, plane)), sem((chunks,)), sem((chunks,)),
            sem((chunks,)), sem((chunks,)), sem((chunks, plane)), sem((chunks, plane)),
        ],
        compiler_params=pltpu.CompilerParams(
            collective_id=0, has_side_effects=True, vmem_limit_bytes=60 * MIB
        ),
        name="correct",
    )(stream, gains.reshape(dets, 1), noise, weights, pattern, *tables)


def bin_kernel(x_ref, row_ref, hit_ref, t4, out_ref, acc_ref, count_ref, rows_ref):
    batch, side, _ = x_ref.shape
    per_row = PIX // side
    tiles = side // per_row
    packed = jnp.concatenate([x_ref[b] for b in range(batch)], axis=1)
    result = product((t4[0], t4[1]), split(packed))
    tiled = []
    for b in range(batch):
        part = result[:, b * side:(b + 1) * side]
        rows_ref[pl.ds(b * side, side), :] = part
        tiled.append(jnp.concatenate([part[p * tiles:(p + 1) * tiles] for p in range(per_row)], axis=1))
    for tile in range(tiles):
        for p in range(per_row):
            at = (tile * per_row + p) * side
            out_ref[:, at:at + side] = rows_ref[pl.ds(p * tiles + tile, batch, stride=side), :]
    high, low = split(jnp.concatenate(tiled, axis=0))
    blocks = acc_ref.shape[0]
    ladder = lax.broadcasted_iota(jnp.int32, (blocks, batch * tiles), 0)
    table = jnp.where(row_ref[...] == ladder, hit_ref[...], 0.0).astype(jnp.bfloat16)
    dot = functools.partial(jnp.dot, preferred_element_type=jnp.float32)
    ones = jnp.ones((8, batch * tiles), jnp.bfloat16)
    counts = lax.dot_general(ones, table, (((1,), (1,)), ((), ())), preferred_element_type=jnp.float32)

    @pl.when(pl.program_id(0) == 0)
    def _():
        acc_ref[...] = jnp.zeros_like(acc_ref)
        count_ref[...] = jnp.zeros_like(count_ref)

    acc_ref[...] += dot(table, high) + dot(table, low)
    count_ref[...] += counts[:1]


def finish_and_bin(packed, rows, hits, table, blocks):
    dets, side, _ = packed.shape
    batch = 8
    tiles = side * side // PIX
    line = pl.BlockSpec((1, batch * tiles), lambda i: (0, i))
    return pl.pallas_call(
        bin_kernel,
        grid=(dets // batch,),
        out_shape=(
            jax.ShapeDtypeStruct((dets, side * side), jnp.float32),
            jax.ShapeDtypeStruct((blocks, PIX), jnp.float32),
            jax.ShapeDtypeStruct((1, blocks), jnp.float32),
        ),
        in_specs=[
            pl.BlockSpec((batch, side, side), lambda i: (i, 0, 0)),
            line,
            line,
            pl.BlockSpec(table.shape, lambda i: (0, 0, 0)),
        ],
        out_specs=(
            pl.BlockSpec((batch, side * side), lambda i: (i, 0)),
            pl.BlockSpec((blocks, PIX), lambda i: (0, 0)),
            pl.BlockSpec((1, blocks), lambda i: (0, 0)),
        ),
        scratch_shapes=[pltpu.VMEM((batch * side, side), jnp.float32)],
        compiler_params=pltpu.CompilerParams(vmem_limit_bytes=48 * MIB),
        name="finish_and_bin",
    )(packed, rows, hits, table)


def map_kernel(size, acc_ref, count_ref, out_ref, landed, tallies, send_sem, recv_sem, tally_send, tally_recv):
    me = lax.axis_index("det")
    rows = out_ref.shape[0]
    barrier = pltpu.get_barrier_semaphore()

    def greet(step, carry):
        pl.semaphore_signal(barrier, inc=1, device_id={"det": lax.rem(me + step, size)})
        return carry

    lax.fori_loop(1, size, greet, 0)
    pl.semaphore_wait(barrier, size - 1)

    def copy(step):
        other = lax.rem(me + step, size)
        return pltpu.make_async_remote_copy(
            src_ref=acc_ref.at[pl.ds(pl.multiple_of(other * rows, 8), rows), :],
            dst_ref=landed.at[step],
            send_sem=send_sem.at[step],
            recv_sem=recv_sem.at[step],
            device_id={"det": other},
        )

    def tally(step):
        return pltpu.make_async_remote_copy(
            src_ref=count_ref,
            dst_ref=tallies.at[step],
            send_sem=tally_send.at[step],
            recv_sem=tally_recv.at[step],
            device_id={"det": lax.rem(me + step, size)},
        )

    def start(step, carry):
        copy(step).start()
        tally(step).start()
        return carry

    lax.fori_loop(1, size, start, 0)

    def add(step, total):
        copy(step).wait_recv()
        tally(step).wait_recv()
        return total[0] + landed[step], total[1] + tallies[step]

    own = acc_ref[pl.ds(pl.multiple_of(me * rows, 8), rows), :]
    sums, counts = lax.fori_loop(1, size, add, (own, count_ref[...]))
    shape = (rows, counts.shape[1])
    mine = lax.broadcasted_iota(jnp.int32, shape, 1) == lax.broadcasted_iota(jnp.int32, shape, 0) + me * rows
    counts = jnp.sum(jnp.where(mine, counts, 0.0), axis=1, keepdims=True)
    out_ref[...] = sums / jnp.sqrt(1.0 + counts)

    def finish(step, carry):
        copy(step).wait_send()
        tally(step).wait_send()
        return carry

    lax.fori_loop(1, size, finish, 0)


def combine_map(acc, counts, size):
    blocks, columns = acc.shape
    rows = blocks // size
    sem = pltpu.SemaphoreType.DMA((size,))
    return pl.pallas_call(
        functools.partial(map_kernel, size),
        out_shape=jax.ShapeDtypeStruct((rows, columns), jnp.float32),
        in_specs=[pl.BlockSpec(memory_space=pltpu.VMEM)] * 2,
        out_specs=pl.BlockSpec(memory_space=pltpu.VMEM),
        scratch_shapes=[
            pltpu.VMEM((size, rows, columns), jnp.float32),
            pltpu.VMEM((size, 1, blocks), jnp.float32),
            sem, sem, sem, sem,
        ],
        compiler_params=pltpu.CompilerParams(collective_id=1, has_side_effects=True),
        name="combine_map",
    )(acc, counts)


def shards(size, timestream, gains, mode_pattern, mode_weights, noise_weight, block_ids, hits, sky_rows):
    items, dets, samples = timestream.shape
    side = math.isqrt(samples)
    ids_flat = block_ids.reshape(-1)
    blocks = sky_rows.shape[0]
    ladder = lax.broadcasted_iota(jnp.int32, (blocks, ids_flat.shape[0]), 0)
    rows = jnp.sum(jnp.where(ids_flat[None, :] == ladder, sky_rows[:, None], 0), axis=0)
    weight = hits.reshape(1, -1).astype(jnp.float32)
    *tables, last = [jnp.asarray(table) for table in transform_tables(side)]
    packed = correct(
        timestream.reshape(items * dets, samples), gains.reshape(-1), noise_weight, mode_pattern, mode_weights,
        tables, size,
    )
    filtered, acc, counts = finish_and_bin(packed.reshape(dets, side, side), rows[None, :], weight, last, blocks)
    return (filtered.reshape(items, dets, samples), combine_map(acc, counts, size))


def solution(mesh):
    in_specs = (
        P("grp", "det", None),
        P("grp", "det"),
        P("grp", None),
        P("grp", None),
        P(("grp", "det"), None),
        P("grp", "det", None),
        P("grp", "det", None),
        P("grp"),
    )
    out_specs = (P("grp", "det", None), P(("grp", "det"), None))
    body = functools.partial(shards, mesh.shape["det"])
    return jax.shard_map(body, mesh=mesh, in_specs=in_specs, out_specs=out_specs, check_vma=False)
```

```python
import functools
import math

import jax
import jax.numpy as jnp
import ml_dtypes
import numpy as np
from jax import lax
from jax.experimental import pallas as pl
from jax.experimental.pallas import tpu as pltpu
from jax.sharding import PartitionSpec as P

PIX = 256
LANES = 128
MIB = 1 << 20


def split(value):
    high = value.astype(jnp.bfloat16)
    return high, (value - high.astype(jnp.float32)).astype(jnp.bfloat16)


def product(left, right):
    dot = functools.partial(jnp.dot, preferred_element_type=jnp.float32)
    return dot(left[0], right[0]) + (dot(left[0], right[1]) + dot(left[1], right[0]))


def halves(table):
    high = table.astype(ml_dtypes.bfloat16)
    low = (table - high.astype(np.float64)).astype(ml_dtypes.bfloat16)
    return np.stack([high, low])


def transform_tables(side):
    index = np.arange(side)
    angle = (np.outer(index, index) % side) * (2.0 * math.pi / side)
    cos, sin = np.cos(angle), np.sin(angle)
    packed = np.stack([cos[: side // 2], -sin[: side // 2]], 1).reshape(side, side)
    packed[1] = cos[side // 2]
    twist = np.outer(np.arange(side // 2 + 1), index) * (2.0 * math.pi / (side * side))
    turn = np.stack([np.cos(twist), np.sin(twist)]).astype(np.float32)
    per_row = PIX // side
    last = packed.T / (side * side)
    last = last.reshape(side // per_row, per_row, side).swapaxes(0, 1).reshape(side, side)
    return (
        halves(packed),
        halves(np.block([[cos, -sin], [sin, cos]])),
        halves(np.block([[cos, sin], [-sin, cos]])),
        np.eye(side)[::-1].astype(ml_dtypes.bfloat16),
        turn,
        halves(last),
    )


def correct_kernel(
    plane, planes, x_ref, gain_ref, noise_hbm, weight_ref, pattern_ref, t1, t2, t3, flip, turn, out_ref,
    noise_ref, noise_sem, cube, cal, slab, part, from_left, from_right, land, fold,
    raw_send, raw_recv, right_send, right_recv, left_send, left_recv, back_send, back_recv,
):
    me = lax.axis_index("det")
    z, q = me // plane, me % plane
    dets, samples = x_ref.shape
    side = t1.shape[1]
    chunks = side // plane
    hop = 2
    lag = hop * (planes - 1)
    mid_lag = max(lag + 2, 8)
    lead = min(4, chunks)
    noise_copy = pltpu.make_async_copy(noise_hbm, noise_ref, noise_sem)
    noise_copy.start()

    barrier = pltpu.get_barrier_semaphore()

    def partner(step):
        return lax.rem(q + step, plane)

    for step in range(1, plane):
        pl.semaphore_signal(barrier, inc=1, device_id={"det": z * plane + partner(step)})

    @pl.when(z > 0)
    def _():
        pl.semaphore_signal(barrier, inc=1, device_id={"det": me - plane})

    @pl.when(z < planes - 1)
    def _():
        pl.semaphore_signal(barrier, inc=1, device_id={"det": me + plane})

    def column(row):
        return pl.ds(pl.multiple_of(row * side, side), side)

    def spread(row):
        return pl.ds(row, dets, stride=side)

    def own_rows(owner):
        return pl.ds(pl.multiple_of(owner * dets, 8), dets)

    def raw_copy(chunk, step):
        other = partner(step)
        return pltpu.make_async_remote_copy(
            src_ref=cal.at[:, column(other * chunks + chunk)],
            dst_ref=slab.at[chunk, own_rows(q), :],
            send_sem=raw_send.at[chunk, step - 1],
            recv_sem=raw_recv.at[chunk, step - 1],
            device_id={"det": z * plane + other},
        )

    def back_copy(chunk, step):
        other = partner(step)
        return pltpu.make_async_remote_copy(
            src_ref=slab.at[chunk, own_rows(other), :],
            dst_ref=land.at[:, column(q * chunks + chunk)],
            send_sem=back_send.at[chunk, step - 1],
            recv_sem=back_recv.at[chunk, step - 1],
            device_id={"det": z * plane + other},
        )

    def right_copy(chunk):
        return pltpu.make_async_remote_copy(
            src_ref=from_left.at[chunk, 1],
            dst_ref=from_left.at[chunk, 0],
            send_sem=right_send.at[chunk],
            recv_sem=right_recv.at[chunk],
            device_id={"det": lax.rem(me + plane, plane * planes)},
        )

    def left_copy(chunk):
        return pltpu.make_async_remote_copy(
            src_ref=from_right.at[chunk, 1],
            dst_ref=from_right.at[chunk, 0],
            send_sem=left_send.at[chunk],
            recv_sem=left_recv.at[chunk],
            device_id={"det": lax.rem(me + plane * (planes - 1), plane * planes)},
        )

    shape = (dets, dets)
    diagonal = lax.broadcasted_iota(jnp.int32, shape, 0) == lax.broadcasted_iota(jnp.int32, shape, 1)
    gain = jnp.sum(jnp.where(diagonal, gain_ref[...], 0.0), axis=1, keepdims=True)
    scale = jnp.broadcast_to(1.0 / gain, (dets, side))

    def to_cube(row, carry):
        cube[spread(row), :] = x_ref[:, column(row)] * scale
        return carry

    lax.fori_loop(0, side, to_cube, 0, unroll=4)
    first_table = (t1[0], t1[1])
    group = 8

    def first_stage(at, carry):
        rows = [pl.ds(pl.multiple_of((at * group + d) * side, side), side) for d in range(group)]
        section = product(first_table, split(jnp.concatenate([cube[row, :] for row in rows], axis=1)))
        for d in range(group):
            cube[rows[d], :] = section[:, d * side:(d + 1) * side]
        return carry

    lax.fori_loop(0, dets // group, first_stage, 0)
    at_ends = (z == 0).astype(jnp.int32) + (z == planes - 1).astype(jnp.int32)
    pl.semaphore_wait(barrier, plane + 1 - at_ends)

    def send_raw(chunk, carry):
        for owner in range(plane):
            row = owner * chunks + chunk
            cal[:, column(row)] = cube[spread(row), :]
        for step in range(1, plane):
            raw_copy(chunk, step).start()
        slab[chunk, own_rows(q), :] = cal[:, column(q * chunks + chunk)]
        return carry

    lax.fori_loop(0, lead, send_raw, 0)
    in_plane = pl.ds(pl.multiple_of(z * plane * dets, 8), plane * dets)
    weight = split(weight_ref[in_plane, :].T)
    pattern = split(pattern_ref[in_plane, :])

    def middle(real, imag, slots):
        turned = []
        for r, m, k in zip(real, imag, slots):
            cos, sin = turn[0, pl.ds(k, 1), :], turn[1, pl.ds(k, 1), :]
            turned.append(jnp.concatenate([r * cos + m * sin, m * cos - r * sin], axis=1))
        freq = product(split(jnp.concatenate(turned, axis=0)), (t2[0], t2[1]))
        weighted = []
        for at, k in enumerate(slots):
            noise = fold[own_rows(k), :]
            weighted.append(freq[at * dets:(at + 1) * dets] * jnp.concatenate([noise, noise], axis=1))
        section = product(split(jnp.concatenate(weighted, axis=0)), (t3[0], t3[1]))
        result = []
        for at, k in enumerate(slots):
            cos, sin = turn[0, pl.ds(k, 1), :], turn[1, pl.ds(k, 1), :]
            r, m = section[at * dets:(at + 1) * dets, :side], section[at * dets:(at + 1) * dets, side:]
            result.append((r * cos - m * sin, m * cos + r * sin))
        return result

    def one_step(i, carry):
        @pl.when(i < chunks)
        def _():
            for step in range(1, plane):
                raw_copy(i, step).wait_recv()
            part[i] = product(weight, split(slab[i]))

        c_right = i - hop * z

        @pl.when((c_right >= 0) & (c_right < chunks))
        def _():
            @pl.when(z == 0)
            def _():
                from_left[c_right, 1] = part[c_right]

            @pl.when(z > 0)
            def _():
                right_copy(c_right).wait_recv()
                from_left[c_right, 1] = part[c_right] + from_left[c_right, 0]

            @pl.when(z < planes - 1)
            def _():
                right_copy(c_right).start()

        c_left = i - hop * (planes - 1 - z)

        @pl.when((c_left >= 0) & (c_left < chunks))
        def _():
            @pl.when(z == planes - 1)
            def _():
                from_right[c_left, 1] = part[c_left]

            @pl.when(z < planes - 1)
            def _():
                left_copy(c_left).wait_recv()
                from_right[c_left, 1] = part[c_left] + from_right[c_left, 0]

            @pl.when(z > 0)
            def _():
                left_copy(c_left).start()

        @pl.when(i + lead < chunks)
        def _():
            send_raw(i + lead, 0)

        c = i - lag

        @pl.when((c >= 0) & (c < chunks))
        def _():
            coeff = from_left[c, 1] + (from_right[c, 1] - part[c])
            slab[c] = slab[c] - product(pattern, split(coeff))
            for step in range(1, plane):
                back_copy(c, step).start()
            land[:, column(q * chunks + c)] = slab[c, own_rows(q), :]

        @pl.when(i == 0)
        def _():
            noise_copy.wait()

        @pl.when(i < 4)
        def _():
            def regroup(at, carry):
                row = i * (side // 4) + at
                out_ref[spread(row), :] = noise_ref[:, column(row)]
                return carry

            lax.fori_loop(0, side // 4, regroup, 0, unroll=4)

        @pl.when((i >= 4) & (i < 8))
        def _():
            def swap(at, carry):
                det = (i - 4) * (dets // 4) + at
                fold[pl.ds(det, side, stride=dets), :] = out_ref[column(det), :].T
                return carry

            lax.fori_loop(0, dets // 4, swap, 0)

        @pl.when(i == 8)
        def _():
            def add_mirror(k, carry):
                high, low = split(fold[own_rows(side - k), :])
                dot = functools.partial(jnp.dot, preferred_element_type=jnp.float32)
                fold[own_rows(k), :] += dot(high, flip[...]) + dot(low, flip[...])
                return carry

            lax.fori_loop(1, side // 2, add_mirror, 0)

        pair = (i - mid_lag - 1) // 2

        @pl.when((i > mid_lag) & ((i - mid_lag) % 2 == 1) & (pair < chunks // 2))
        def _():
            for step in range(1, plane):
                back_copy(2 * pair, step).wait_recv()
                back_copy(2 * pair + 1, step).wait_recv()
            slots = [owner * (chunks // 2) + pair for owner in range(plane)]
            real = [land[:, column(2 * k)] for k in slots]
            imag = [land[:, column(2 * k + 1)] for k in slots]
            for k, (r, m) in zip(slots, middle(real, imag, slots)):
                out_ref[spread(2 * k), :] = r
                out_ref[spread(2 * k + 1), :] = m

            @pl.when(pair == 0)
            def _():
                none = jnp.zeros((dets, side), jnp.float32)
                ends = middle([real[0], imag[0]], [none, none], [0, side // 2])
                out_ref[spread(0), :] = ends[0][0]
                out_ref[spread(1), :] = ends[1][0]

        return carry

    lax.fori_loop(0, chunks + mid_lag + 1, one_step, 0)

    def finish(chunk, carry):
        for step in range(1, plane):
            back_copy(chunk, step).wait_send()
            raw_copy(chunk, step).wait_send()

        @pl.when(z < planes - 1)
        def _():
            right_copy(chunk).wait_send()

        @pl.when(z > 0)
        def _():
            left_copy(chunk).wait_send()

        return carry

    lax.fori_loop(0, chunks, finish, 0)


def correct(stream, gains, noise, mode_pattern, mode_weights, tables, size):
    dets, samples = stream.shape
    rank = mode_pattern.shape[1]
    side = math.isqrt(samples)
    plane = 4 if size % 4 == 0 else 1
    planes = size // plane
    chunks = side // plane
    rows = plane * dets
    f32 = jnp.float32
    vmem = pl.BlockSpec(memory_space=pltpu.VMEM)
    sem = pltpu.SemaphoreType.DMA
    coeffs = pltpu.VMEM((chunks, rank, side), f32)
    chain = pltpu.VMEM((chunks, 2, rank, side), f32)
    whole = pltpu.VMEM((dets, samples), f32)
    cube = pltpu.VMEM((dets * side, side), f32)
    return pl.pallas_call(
        functools.partial(correct_kernel, plane, planes),
        out_shape=jax.ShapeDtypeStruct((dets * side, side), f32),
        in_specs=[vmem, vmem, pl.BlockSpec(memory_space=pl.ANY)] + [vmem] * (2 + len(tables)),
        out_specs=pl.BlockSpec(memory_space=pltpu.VMEM),
        scratch_shapes=[
            whole, sem(()), cube, whole, pltpu.VMEM((chunks, rows, side), f32), coeffs, chain, chain, whole, cube,
            sem((chunks, plane)), sem((chunks, plane)), sem((chunks,)), sem((chunks,)),
            sem((chunks,)), sem((chunks,)), sem((chunks, plane)), sem((chunks, plane)),
        ],
        compiler_params=pltpu.CompilerParams(
            collective_id=0, has_side_effects=True, vmem_limit_bytes=60 * MIB
        ),
        name="correct",
    )(stream, gains, noise, mode_weights, mode_pattern, *tables)


def bin_kernel(x_ref, id_ref, hit_ref, sky_ref, t4, out_ref, acc_ref, count_ref, rows_ref):
    batch, side, _ = x_ref.shape
    per_row = PIX // side
    tiles = side // per_row
    packed = jnp.concatenate([x_ref[b] for b in range(batch)], axis=1)
    result = product((t4[0], t4[1]), split(packed))
    tiled = []
    for b in range(batch):
        part = result[:, b * side:(b + 1) * side]
        rows_ref[pl.ds(b * side, side), :] = part
        tiled.append(jnp.concatenate([part[p * tiles:(p + 1) * tiles] for p in range(per_row)], axis=1))
    for tile in range(tiles):
        for p in range(per_row):
            at = (tile * per_row + p) * side
            out_ref[:, at:at + side] = rows_ref[pl.ds(p * tiles + tile, batch, stride=side), :]
    high, low = split(jnp.concatenate(tiled, axis=0))
    blocks = acc_ref.shape[0]
    ladder = lax.broadcasted_iota(jnp.int32, (blocks, batch * tiles), 0)
    ids = jnp.concatenate([id_ref[b:b + 1, :] for b in range(batch)], axis=1)
    hits = jnp.concatenate([hit_ref[b:b + 1, :] for b in range(batch)], axis=1).astype(jnp.float32)
    table = jnp.where(ids == ladder, hits, 0.0).astype(jnp.bfloat16)
    dot = functools.partial(jnp.dot, preferred_element_type=jnp.float32)
    ones = jnp.ones((8, batch * tiles), jnp.bfloat16)
    counts = lax.dot_general(ones, table, (((1,), (1,)), ((), ())), preferred_element_type=jnp.float32)

    @pl.when(pl.program_id(0) == 0)
    def _():
        acc_ref[...] = jnp.zeros_like(acc_ref)
        count_ref[...] = jnp.zeros_like(count_ref)

    acc_ref[...] += dot(table, high) + dot(table, low)
    count_ref[...] += counts[:1]

    @pl.when(pl.program_id(0) == pl.num_programs(0) - 1)
    def _():
        ladder = lax.broadcasted_iota(jnp.int32, (blocks, blocks), 0)
        place = jnp.where(sky_ref[...] == ladder, 1.0, 0.0).astype(jnp.bfloat16)
        total = acc_ref[...]
        high, low = split(total)
        rest = (total - high.astype(jnp.float32) - low.astype(jnp.float32)).astype(jnp.bfloat16)
        acc_ref[...] = dot(place, high) + (dot(place, low) + dot(place, rest))
        tally = jnp.broadcast_to(count_ref[...], (8, blocks))
        across = functools.partial(
            lax.dot_general, dimension_numbers=(((1,), (1,)), ((), ())), preferred_element_type=jnp.float32
        )
        high, low = split(tally)
        count_ref[...] = (across(high, place) + across(low, place))[:1]


def finish_and_bin(packed, ids, hits, sky_rows, table):
    dets, side, _ = packed.shape
    batch = 8
    tiles = side * side // PIX
    blocks = sky_rows.shape[1]
    line = pl.BlockSpec((batch, tiles), lambda i: (i, 0))
    return pl.pallas_call(
        bin_kernel,
        grid=(dets // batch,),
        out_shape=(
            jax.ShapeDtypeStruct((dets, side * side), jnp.float32),
            jax.ShapeDtypeStruct((blocks, PIX), jnp.float32),
            jax.ShapeDtypeStruct((1, blocks), jnp.float32),
        ),
        in_specs=[
            pl.BlockSpec((batch, side, side), lambda i: (i, 0, 0)),
            line,
            line,
            pl.BlockSpec((1, blocks), lambda i: (0, 0)),
            pl.BlockSpec(table.shape, lambda i: (0, 0, 0)),
        ],
        out_specs=(
            pl.BlockSpec((batch, side * side), lambda i: (i, 0)),
            pl.BlockSpec((blocks, PIX), lambda i: (0, 0)),
            pl.BlockSpec((1, blocks), lambda i: (0, 0)),
        ),
        scratch_shapes=[pltpu.VMEM((batch * side, side), jnp.float32)],
        compiler_params=pltpu.CompilerParams(vmem_limit_bytes=60 * MIB),
        name="finish_and_bin",
    )(packed, ids, hits, sky_rows, table)


def map_kernel(size, acc_ref, count_ref, out_ref, landed, tallies, send_sem, recv_sem, tally_send, tally_recv):
    me = lax.axis_index("det")
    rows = out_ref.shape[0]
    barrier = pltpu.get_barrier_semaphore()

    def greet(step, carry):
        pl.semaphore_signal(barrier, inc=1, device_id={"det": lax.rem(me + step, size)})
        return carry

    lax.fori_loop(1, size, greet, 0)
    pl.semaphore_wait(barrier, size - 1)

    def copy(step):
        other = lax.rem(me + step, size)
        return pltpu.make_async_remote_copy(
            src_ref=acc_ref.at[pl.ds(pl.multiple_of(other * rows, 8), rows), :],
            dst_ref=landed.at[step],
            send_sem=send_sem.at[step],
            recv_sem=recv_sem.at[step],
            device_id={"det": other},
        )

    def tally(step):
        return pltpu.make_async_remote_copy(
            src_ref=count_ref,
            dst_ref=tallies.at[step],
            send_sem=tally_send.at[step],
            recv_sem=tally_recv.at[step],
            device_id={"det": lax.rem(me + step, size)},
        )

    def start(step, carry):
        copy(step).start()
        tally(step).start()
        return carry

    lax.fori_loop(1, size, start, 0)

    def add(step, total):
        copy(step).wait_recv()
        tally(step).wait_recv()
        return total[0] + landed[step], total[1] + tallies[step]

    own = acc_ref[pl.ds(pl.multiple_of(me * rows, 8), rows), :]
    sums, counts = lax.fori_loop(1, size, add, (own, count_ref[...]))
    shape = (rows, counts.shape[1])
    mine = lax.broadcasted_iota(jnp.int32, shape, 1) == lax.broadcasted_iota(jnp.int32, shape, 0) + me * rows
    counts = jnp.sum(jnp.where(mine, counts, 0.0), axis=1, keepdims=True)
    out_ref[...] = sums / jnp.sqrt(1.0 + counts)

    def finish(step, carry):
        copy(step).wait_send()
        tally(step).wait_send()
        return carry

    lax.fori_loop(1, size, finish, 0)


def combine_map(acc, counts, size):
    blocks, columns = acc.shape
    rows = blocks // size
    sem = pltpu.SemaphoreType.DMA((size,))
    return pl.pallas_call(
        functools.partial(map_kernel, size),
        out_shape=jax.ShapeDtypeStruct((rows, columns), jnp.float32),
        in_specs=[pl.BlockSpec(memory_space=pltpu.VMEM)] * 2,
        out_specs=pl.BlockSpec(memory_space=pltpu.VMEM),
        scratch_shapes=[
            pltpu.VMEM((size, rows, columns), jnp.float32),
            pltpu.VMEM((size, 1, blocks), jnp.float32),
            sem, sem, sem, sem,
        ],
        compiler_params=pltpu.CompilerParams(collective_id=1, has_side_effects=True),
        name="combine_map",
    )(acc, counts)


def shards(size, timestream, gains, mode_pattern, mode_weights, noise_weight, block_ids, hits, sky_rows):
    items, dets, samples = timestream.shape
    side = math.isqrt(samples)
    *tables, last = [jnp.asarray(table) for table in transform_tables(side)]
    packed = correct(
        timestream.reshape(items * dets, samples), gains, noise_weight, mode_pattern, mode_weights,
        tables, size,
    )
    filtered, acc, counts = finish_and_bin(
        packed.reshape(dets, side, side), block_ids.reshape(dets, -1), hits.reshape(dets, -1), sky_rows[None, :], last
    )
    return (filtered.reshape(items, dets, samples), combine_map(acc, counts, size))


def solution(mesh):
    in_specs = (
        P("grp", "det", None),
        P("grp", "det"),
        P("grp", None),
        P("grp", None),
        P(("grp", "det"), None),
        P("grp", "det", None),
        P("grp", "det", None),
        P("grp"),
    )
    out_specs = (P("grp", "det", None), P(("grp", "det"), None))
    body = functools.partial(shards, mesh.shape["det"])
    return jax.shard_map(body, mesh=mesh, in_specs=in_specs, out_specs=out_specs, check_vma=False)
```

```python
import functools
import math

import jax
import jax.numpy as jnp
import ml_dtypes
import numpy as np
from jax import lax
from jax.experimental import pallas as pl
from jax.experimental.pallas import tpu as pltpu
from jax.sharding import PartitionSpec as P

PIX = 256
LANES = 128
MIB = 1 << 20


def split(value):
    high = value.astype(jnp.bfloat16)
    return high, (value - high.astype(jnp.float32)).astype(jnp.bfloat16)


def product(left, right):
    dot = functools.partial(jnp.dot, preferred_element_type=jnp.float32)
    return dot(left[0], right[0]) + (dot(left[0], right[1]) + dot(left[1], right[0]))


def halves(table):
    high = table.astype(ml_dtypes.bfloat16)
    low = (table - high.astype(np.float64)).astype(ml_dtypes.bfloat16)
    return np.stack([high, low])


def transform_tables(side):
    index = np.arange(side)
    angle = (np.outer(index, index) % side) * (2.0 * math.pi / side)
    cos, sin = np.cos(angle), np.sin(angle)
    packed = np.stack([cos[: side // 2], -sin[: side // 2]], 1).reshape(side, side)
    packed[1] = cos[side // 2]
    twist = np.outer(np.arange(side // 2 + 1), index) * (2.0 * math.pi / (side * side))
    turn = np.stack([np.cos(twist), np.sin(twist)]).astype(np.float32)
    per_row = PIX // side
    last = packed.T / (side * side)
    last = last.reshape(side // per_row, per_row, side).swapaxes(0, 1).reshape(side, side)
    return (
        halves(packed),
        halves(np.block([[cos, -sin], [sin, cos]])),
        halves(np.block([[cos, sin], [-sin, cos]])),
        np.eye(side)[::-1].astype(ml_dtypes.bfloat16),
        turn,
        halves(last),
    )


def correct_kernel(
    plane, planes, x_ref, gain_ref, noise_hbm, weight_ref, pattern_ref, t1, t2, t3, flip, turn, out_ref,
    noise_ref, noise_sem, cube, cal, slab, part, from_left, from_right, land, fold,
    raw_send, raw_recv, right_send, right_recv, left_send, left_recv, back_send, back_recv,
):
    me = lax.axis_index("det")
    z, q = me // plane, me % plane
    dets, samples = x_ref.shape
    side = t1.shape[1]
    pairs = side // plane // 2
    rank = part.shape[1]
    lag = planes - 1
    mid_lag = max(lag + 1, 4)
    lead = min(3, pairs)
    noise_copy = pltpu.make_async_copy(noise_hbm, noise_ref, noise_sem)
    noise_copy.start()

    barrier = pltpu.get_barrier_semaphore()

    def partner(step):
        return lax.rem(q + step, plane)

    for step in range(1, plane):
        pl.semaphore_signal(barrier, inc=1, device_id={"det": z * plane + partner(step)})

    @pl.when(z > 0)
    def _():
        pl.semaphore_signal(barrier, inc=1, device_id={"det": me - plane})

    @pl.when(z < planes - 1)
    def _():
        pl.semaphore_signal(barrier, inc=1, device_id={"det": me + plane})

    def column(row):
        return pl.ds(pl.multiple_of(row * side, side), side)

    def slot(k):
        return pl.ds(pl.multiple_of(k * 2 * side, 2 * side), 2 * side)

    def spread(row):
        return pl.ds(row, dets, stride=side)

    def own_rows(owner):
        return pl.ds(pl.multiple_of(owner * dets, 8), dets)

    def raw_copy(pair, step):
        other = partner(step)
        return pltpu.make_async_remote_copy(
            src_ref=cal.at[:, slot(other * pairs + pair)],
            dst_ref=slab.at[pair, own_rows(q), :],
            send_sem=raw_send.at[pair, step - 1],
            recv_sem=raw_recv.at[pair, step - 1],
            device_id={"det": z * plane + other},
        )

    def back_copy(pair, step):
        other = partner(step)
        return pltpu.make_async_remote_copy(
            src_ref=slab.at[pair, own_rows(other), :],
            dst_ref=land.at[:, slot(q * pairs + pair)],
            send_sem=back_send.at[pair, step - 1],
            recv_sem=back_recv.at[pair, step - 1],
            device_id={"det": z * plane + other},
        )

    halves_of = [pl.ds(h * (rank // 2), rank // 2) for h in range(2)]

    def right_copy(pair, h):
        return pltpu.make_async_remote_copy(
            src_ref=from_left.at[pair, 1, halves_of[h], :],
            dst_ref=from_left.at[pair, 0, halves_of[h], :],
            send_sem=right_send.at[pair, h],
            recv_sem=right_recv.at[pair, h],
            device_id={"det": lax.rem(me + plane, plane * planes)},
        )

    def left_copy(pair, h):
        return pltpu.make_async_remote_copy(
            src_ref=from_right.at[pair, 1, halves_of[h], :],
            dst_ref=from_right.at[pair, 0, halves_of[h], :],
            send_sem=left_send.at[pair, h],
            recv_sem=left_recv.at[pair, h],
            device_id={"det": lax.rem(me + plane * (planes - 1), plane * planes)},
        )

    shape = (dets, dets)
    diagonal = lax.broadcasted_iota(jnp.int32, shape, 0) == lax.broadcasted_iota(jnp.int32, shape, 1)
    gain = jnp.sum(jnp.where(diagonal, gain_ref[...], 0.0), axis=1, keepdims=True)
    scale = jnp.broadcast_to(1.0 / gain, (dets, side))

    def to_cube(row, carry):
        cube[spread(row), :] = x_ref[:, column(row)] * scale
        return carry

    lax.fori_loop(0, side, to_cube, 0, unroll=8)
    first_table = (t1[0], t1[1])
    group = 8

    def first_stage(at, carry):
        rows = [pl.ds(pl.multiple_of((at * group + d) * side, side), side) for d in range(group)]
        section = product(first_table, split(jnp.concatenate([cube[row, :] for row in rows], axis=1)))
        for d in range(group):
            cube[rows[d], :] = section[:, d * side:(d + 1) * side]
        return carry

    lax.fori_loop(0, dets // group, first_stage, 0)
    at_ends = (z == 0).astype(jnp.int32) + (z == planes - 1).astype(jnp.int32)
    pl.semaphore_wait(barrier, plane + 1 - at_ends)

    def send_raw(pair, carry):
        for owner in range(plane):
            k = owner * pairs + pair
            cal[:, column(2 * k)] = cube[spread(2 * k), :]
            cal[:, column(2 * k + 1)] = cube[spread(2 * k + 1), :]
        for step in range(1, plane):
            raw_copy(pair, step).start()
        slab[pair, own_rows(q), :] = cal[:, slot(q * pairs + pair)]
        return carry

    lax.fori_loop(0, lead, send_raw, 0)
    in_plane = pl.ds(pl.multiple_of(z * plane * dets, 8), plane * dets)
    weight = split(weight_ref[in_plane, :].T)
    pattern = split(pattern_ref[in_plane, :])

    def measure_modes(pair):
        for step in range(1, plane):
            raw_copy(pair, step).wait_recv()
        part[pair] = product(weight, split(slab[pair]))

    measure_modes(0)

    def middle(real, imag, slots):
        turned = []
        for r, m, k in zip(real, imag, slots):
            cos, sin = turn[0, pl.ds(k, 1), :], turn[1, pl.ds(k, 1), :]
            turned.append(jnp.concatenate([r * cos + m * sin, m * cos - r * sin], axis=1))
        freq = product(split(jnp.concatenate(turned, axis=0)), (t2[0], t2[1]))
        weighted = []
        for at, k in enumerate(slots):
            noise = fold[own_rows(k), :]
            weighted.append(freq[at * dets:(at + 1) * dets] * jnp.concatenate([noise, noise], axis=1))
        section = product(split(jnp.concatenate(weighted, axis=0)), (t3[0], t3[1]))
        result = []
        for at, k in enumerate(slots):
            cos, sin = turn[0, pl.ds(k, 1), :], turn[1, pl.ds(k, 1), :]
            r, m = section[at * dets:(at + 1) * dets, :side], section[at * dets:(at + 1) * dets, side:]
            result.append((r * cos - m * sin, m * cos + r * sin))
        return result

    def one_step(i, carry):
        c_right = i - z
        c_left = i - (planes - 1 - z)
        for h in range(2):
            rows = halves_of[h]

            @pl.when((c_right >= 0) & (c_right < pairs))
            def _():
                @pl.when(z == 0)
                def _():
                    from_left[c_right, 1, rows, :] = part[c_right, rows, :]

                @pl.when(z > 0)
                def _():
                    right_copy(c_right, h).wait_recv()
                    from_left[c_right, 1, rows, :] = part[c_right, rows, :] + from_left[c_right, 0, rows, :]

                @pl.when(z < planes - 1)
                def _():
                    right_copy(c_right, h).start()

            @pl.when((c_left >= 0) & (c_left < pairs))
            def _():
                @pl.when(z == planes - 1)
                def _():
                    from_right[c_left, 1, rows, :] = part[c_left, rows, :]

                @pl.when(z < planes - 1)
                def _():
                    left_copy(c_left, h).wait_recv()
                    from_right[c_left, 1, rows, :] = part[c_left, rows, :] + from_right[c_left, 0, rows, :]

                @pl.when(z > 0)
                def _():
                    left_copy(c_left, h).start()

        @pl.when(i + lead < pairs)
        def _():
            send_raw(i + lead, 0)

        c = i - lag

        @pl.when((c >= 0) & (c < pairs))
        def _():
            coeff = from_left[c, 1] + (from_right[c, 1] - part[c])
            slab[c] = slab[c] - product(pattern, split(coeff))
            for step in range(1, plane):
                back_copy(c, step).start()
            land[:, slot(q * pairs + c)] = slab[c, own_rows(q), :]

        @pl.when(i + 1 < pairs)
        def _():
            measure_modes(i + 1)

        @pl.when(i == 0)
        def _():
            noise_copy.wait()

        @pl.when(i < 2)
        def _():
            def regroup(at, carry):
                row = i * (side // 2) + at
                out_ref[spread(row), :] = noise_ref[:, column(row)]
                return carry

            lax.fori_loop(0, side // 2, regroup, 0, unroll=4)

        @pl.when((i >= 2) & (i < 4))
        def _():
            def swap(at, carry):
                det = (i - 2) * (dets // 2) + at
                fold[pl.ds(det, side, stride=dets), :] = out_ref[column(det), :].T
                return carry

            lax.fori_loop(0, dets // 2, swap, 0, unroll=2)

        @pl.when(i == 3)
        def _():
            def add_mirror(at, carry):
                ks = [1 + at * 3 + j for j in range(3)]
                high, low = split(jnp.concatenate([fold[own_rows(side - k), :] for k in ks], axis=0))
                dot = functools.partial(jnp.dot, preferred_element_type=jnp.float32)
                mirror = dot(high, flip[...]) + dot(low, flip[...])
                for j, k in enumerate(ks):
                    fold[own_rows(k), :] += mirror[j * dets:(j + 1) * dets]
                return carry

            lax.fori_loop(0, (side // 2 - 1) // 3, add_mirror, 0)

        pair = i - mid_lag

        @pl.when((pair >= 0) & (pair < pairs))
        def _():
            for step in range(1, plane):
                back_copy(pair, step).wait_recv()
            slots = [owner * pairs + pair for owner in range(plane)]
            real = [land[:, column(2 * k)] for k in slots]
            imag = [land[:, column(2 * k + 1)] for k in slots]
            for k, (r, m) in zip(slots, middle(real, imag, slots)):
                out_ref[spread(2 * k), :] = r
                out_ref[spread(2 * k + 1), :] = m

            @pl.when(pair == 0)
            def _():
                none = jnp.zeros((dets, side), jnp.float32)
                ends = middle([real[0], imag[0]], [none, none], [0, side // 2])
                out_ref[spread(0), :] = ends[0][0]
                out_ref[spread(1), :] = ends[1][0]

        return carry

    lax.fori_loop(0, pairs + mid_lag, one_step, 0)

    def finish(pair, carry):
        for step in range(1, plane):
            back_copy(pair, step).wait_send()
            raw_copy(pair, step).wait_send()

        @pl.when(z < planes - 1)
        def _():
            for h in range(2):
                right_copy(pair, h).wait_send()

        @pl.when(z > 0)
        def _():
            for h in range(2):
                left_copy(pair, h).wait_send()

        return carry

    lax.fori_loop(0, pairs, finish, 0)


def correct(stream, gains, noise, mode_pattern, mode_weights, tables, size):
    dets, samples = stream.shape
    rank = mode_pattern.shape[1]
    side = math.isqrt(samples)
    plane = 4 if size % 4 == 0 else 1
    planes = size // plane
    pairs = side // plane // 2
    rows = plane * dets
    f32 = jnp.float32
    vmem = pl.BlockSpec(memory_space=pltpu.VMEM)
    sem = pltpu.SemaphoreType.DMA
    coeffs = pltpu.VMEM((pairs, rank, 2 * side), f32)
    chain = pltpu.VMEM((pairs, 2, rank, 2 * side), f32)
    whole = pltpu.VMEM((dets, samples), f32)
    cube = pltpu.VMEM((dets * side, side), f32)
    return pl.pallas_call(
        functools.partial(correct_kernel, plane, planes),
        out_shape=jax.ShapeDtypeStruct((dets * side, side), f32),
        in_specs=[vmem, vmem, pl.BlockSpec(memory_space=pl.ANY)] + [vmem] * (2 + len(tables)),
        out_specs=pl.BlockSpec(memory_space=pltpu.VMEM),
        scratch_shapes=[
            whole, sem(()), cube, whole, pltpu.VMEM((pairs, rows, 2 * side), f32), coeffs, chain, chain, whole, cube,
            sem((pairs, plane)), sem((pairs, plane)), sem((pairs, 2)), sem((pairs, 2)),
            sem((pairs, 2)), sem((pairs, 2)), sem((pairs, plane)), sem((pairs, plane)),
        ],
        compiler_params=pltpu.CompilerParams(
            collective_id=0, has_side_effects=True, vmem_limit_bytes=60 * MIB
        ),
        name="correct",
    )(stream, gains, noise, mode_weights, mode_pattern, *tables)


def bin_kernel(x_ref, id_ref, hit_ref, sky_ref, t4, out_ref, acc_ref, count_ref, rows_ref):
    batch, side, _ = x_ref.shape
    per_row = PIX // side
    tiles = side // per_row
    packed = jnp.concatenate([x_ref[b] for b in range(batch)], axis=1)
    result = product((t4[0], t4[1]), split(packed))
    tiled = []
    for b in range(batch):
        part = result[:, b * side:(b + 1) * side]
        rows_ref[pl.ds(b * side, side), :] = part
        tiled.append(jnp.concatenate([part[p * tiles:(p + 1) * tiles] for p in range(per_row)], axis=1))
    for tile in range(tiles):
        for p in range(per_row):
            at = (tile * per_row + p) * side
            out_ref[:, at:at + side] = rows_ref[pl.ds(p * tiles + tile, batch, stride=side), :]
    high, low = split(jnp.concatenate(tiled, axis=0))
    blocks = acc_ref.shape[0]
    ladder = lax.broadcasted_iota(jnp.int32, (blocks, batch * tiles), 0)
    ids = jnp.concatenate([id_ref[b:b + 1, :] for b in range(batch)], axis=1)
    hits = jnp.concatenate([hit_ref[b:b + 1, :] for b in range(batch)], axis=1).astype(jnp.float32)
    table = jnp.where(ids == ladder, hits, 0.0).astype(jnp.bfloat16)
    dot = functools.partial(jnp.dot, preferred_element_type=jnp.float32)
    ones = jnp.ones((8, batch * tiles), jnp.bfloat16)
    counts = lax.dot_general(ones, table, (((1,), (1,)), ((), ())), preferred_element_type=jnp.float32)

    @pl.when(pl.program_id(0) == 0)
    def _():
        acc_ref[...] = jnp.zeros_like(acc_ref)
        count_ref[...] = jnp.zeros_like(count_ref)

    acc_ref[...] += dot(table, high) + dot(table, low)
    count_ref[...] += counts[:1]

    @pl.when(pl.program_id(0) == pl.num_programs(0) - 1)
    def _():
        ladder = lax.broadcasted_iota(jnp.int32, (blocks, blocks), 0)
        place = jnp.where(sky_ref[...] == ladder, 1.0, 0.0).astype(jnp.bfloat16)
        total = acc_ref[...]
        high, low = split(total)
        rest = (total - high.astype(jnp.float32) - low.astype(jnp.float32)).astype(jnp.bfloat16)
        acc_ref[...] = dot(place, high) + (dot(place, low) + dot(place, rest))
        tally = jnp.broadcast_to(count_ref[...], (8, blocks))
        across = functools.partial(
            lax.dot_general, dimension_numbers=(((1,), (1,)), ((), ())), preferred_element_type=jnp.float32
        )
        high, low = split(tally)
        count_ref[...] = (across(high, place) + across(low, place))[:1]


def finish_and_bin(packed, ids, hits, sky_rows, table):
    dets, side, _ = packed.shape
    batch = 8
    tiles = side * side // PIX
    blocks = sky_rows.shape[1]
    line = pl.BlockSpec((batch, tiles), lambda i: (i, 0))
    return pl.pallas_call(
        bin_kernel,
        grid=(dets // batch,),
        out_shape=(
            jax.ShapeDtypeStruct((dets, side * side), jnp.float32),
            jax.ShapeDtypeStruct((blocks, PIX), jnp.float32),
            jax.ShapeDtypeStruct((1, blocks), jnp.float32),
        ),
        in_specs=[
            pl.BlockSpec((batch, side, side), lambda i: (i, 0, 0)),
            line,
            line,
            pl.BlockSpec((1, blocks), lambda i: (0, 0)),
            pl.BlockSpec(table.shape, lambda i: (0, 0, 0)),
        ],
        out_specs=(
            pl.BlockSpec((batch, side * side), lambda i: (i, 0)),
            pl.BlockSpec((blocks, PIX), lambda i: (0, 0)),
            pl.BlockSpec((1, blocks), lambda i: (0, 0)),
        ),
        scratch_shapes=[pltpu.VMEM((batch * side, side), jnp.float32)],
        compiler_params=pltpu.CompilerParams(vmem_limit_bytes=60 * MIB),
        name="finish_and_bin",
    )(packed, ids, hits, sky_rows, table)


def map_kernel(
    plane, planes, acc_ref, count_ref, out_ref,
    near, near_tally, partial, tally, far, far_tally,
    near_send, near_recv, near_tally_send, near_tally_recv, far_send, far_recv, far_tally_send, far_tally_recv,
):
    me = lax.axis_index("det")
    z, q = me // plane, me % plane
    rows, columns = out_ref.shape
    barrier = pltpu.get_barrier_semaphore()

    def neighbour(step):
        return z * plane + lax.rem(q + step, plane)

    def beyond(step):
        return lax.rem(me + step * plane, plane * planes)

    for step in range(1, plane):
        pl.semaphore_signal(barrier, inc=1, device_id={"det": neighbour(step)})
    for step in range(1, planes):
        pl.semaphore_signal(barrier, inc=1, device_id={"det": beyond(step)})
    pl.semaphore_wait(barrier, plane + planes - 2)

    def share(owner):
        return pl.ds(pl.multiple_of(owner * rows, 8), rows)

    def remote(source, target, send_sem, recv_sem, device):
        return pltpu.make_async_remote_copy(
            src_ref=source, dst_ref=target, send_sem=send_sem, recv_sem=recv_sem, device_id={"det": device}
        )

    first, second = [], []
    for step in range(1, plane):
        source = acc_ref.at[:, share(lax.rem(q + step, plane)), :]
        at = step - 1
        first.append((
            remote(source, near.at[at], near_send.at[at], near_recv.at[at], neighbour(step)),
            remote(count_ref, near_tally.at[at], near_tally_send.at[at], near_tally_recv.at[at], neighbour(step)),
        ))
    for step in range(1, planes):
        at = step - 1
        source = partial.at[lax.rem(z + step, planes)]
        second.append((
            remote(source, far.at[at], far_send.at[at], far_recv.at[at], beyond(step)),
            remote(tally, far_tally.at[at], far_tally_send.at[at], far_tally_recv.at[at], beyond(step)),
        ))
    for pair in first:
        for copy in pair:
            copy.start()
    sums, counts = acc_ref[:, share(q), :], count_ref[...]
    for at, pair in enumerate(first):
        for copy in pair:
            copy.wait_recv()
        sums, counts = sums + near[at], counts + near_tally[at]
    partial[...] = sums
    tally[...] = counts
    for pair in second:
        for copy in pair:
            copy.start()
    sums = partial[z]
    for at, pair in enumerate(second):
        for copy in pair:
            copy.wait_recv()
        sums, counts = sums + far[at], counts + far_tally[at]
    shape = (rows, counts.shape[1])
    mine = lax.broadcasted_iota(jnp.int32, shape, 1) == lax.broadcasted_iota(jnp.int32, shape, 0) + me * rows
    counts = jnp.sum(jnp.where(mine, counts, 0.0), axis=1, keepdims=True)
    out_ref[...] = sums / jnp.sqrt(1.0 + counts)
    for pair in first + second:
        for copy in pair:
            copy.wait_send()


def combine_map(acc, counts, size):
    blocks, columns = acc.shape
    rows = blocks // size
    plane = 4 if size % 4 == 0 else 1
    planes = size // plane
    near, far = max(1, plane - 1), max(1, planes - 1)
    sems = [pltpu.SemaphoreType.DMA((near,))] * 4 + [pltpu.SemaphoreType.DMA((far,))] * 4
    f32 = jnp.float32
    return pl.pallas_call(
        functools.partial(map_kernel, plane, planes),
        out_shape=jax.ShapeDtypeStruct((rows, columns), f32),
        in_specs=[pl.BlockSpec(memory_space=pltpu.VMEM)] * 2,
        out_specs=pl.BlockSpec(memory_space=pltpu.VMEM),
        scratch_shapes=[
            pltpu.VMEM((near, planes, rows, columns), f32),
            pltpu.VMEM((near, 1, blocks), f32),
            pltpu.VMEM((planes, rows, columns), f32),
            pltpu.VMEM((1, blocks), f32),
            pltpu.VMEM((far, rows, columns), f32),
            pltpu.VMEM((far, 1, blocks), f32),
            *sems,
        ],
        compiler_params=pltpu.CompilerParams(collective_id=1, has_side_effects=True),
        name="combine_map",
    )(acc.reshape(planes, plane * rows, columns), counts)


def shards(size, timestream, gains, mode_pattern, mode_weights, noise_weight, block_ids, hits, sky_rows):
    items, dets, samples = timestream.shape
    side = math.isqrt(samples)
    *tables, last = [jnp.asarray(table) for table in transform_tables(side)]
    packed = correct(
        timestream.reshape(items * dets, samples), gains, noise_weight, mode_pattern, mode_weights,
        tables, size,
    )
    filtered, acc, counts = finish_and_bin(
        packed.reshape(dets, side, side), block_ids.reshape(dets, -1), hits.reshape(dets, -1), sky_rows[None, :], last
    )
    return (filtered.reshape(items, dets, samples), combine_map(acc, counts, size))


def solution(mesh):
    in_specs = (
        P("grp", "det", None),
        P("grp", "det"),
        P("grp", None),
        P("grp", None),
        P(("grp", "det"), None),
        P("grp", "det", None),
        P("grp", "det", None),
        P("grp"),
    )
    out_specs = (P("grp", "det", None), P(("grp", "det"), None))
    body = functools.partial(shards, mesh.shape["det"])
    return jax.shard_map(body, mesh=mesh, in_specs=in_specs, out_specs=out_specs, check_vma=False)
```

```python
import functools
import math

import jax
import jax.numpy as jnp
import ml_dtypes
import numpy as np
from jax import lax
from jax.experimental import pallas as pl
from jax.experimental.pallas import tpu as pltpu
from jax.sharding import PartitionSpec as P

PIX = 256
LANES = 128
MIB = 1 << 20


def split(value):
    high = value.astype(jnp.bfloat16)
    return high, (value - high.astype(jnp.float32)).astype(jnp.bfloat16)


def product(left, right):
    dot = functools.partial(jnp.dot, preferred_element_type=jnp.float32)
    return dot(left[0], right[0]) + (dot(left[0], right[1]) + dot(left[1], right[0]))


def halves(table):
    high = table.astype(ml_dtypes.bfloat16)
    low = (table - high.astype(np.float64)).astype(ml_dtypes.bfloat16)
    return np.stack([high, low])


def transform_tables(side):
    index = np.arange(side)
    angle = (np.outer(index, index) % side) * (2.0 * math.pi / side)
    cos, sin = np.cos(angle), np.sin(angle)
    packed = np.stack([cos[: side // 2], -sin[: side // 2]], 1).reshape(side, side)
    packed[1] = cos[side // 2]
    twist = np.outer(np.arange(side // 2 + 1), index) * (2.0 * math.pi / (side * side))
    turn = np.stack([np.cos(twist), np.sin(twist)]).astype(np.float32)
    per_row = PIX // side
    last = packed.T / (side * side)
    last = last.reshape(side // per_row, per_row, side).swapaxes(0, 1).reshape(side, side)
    return (
        halves(packed),
        halves(np.block([[cos, -sin], [sin, cos]])),
        halves(np.block([[cos, sin], [-sin, cos]])),
        np.eye(side)[::-1].astype(ml_dtypes.bfloat16),
        turn,
        halves(last),
    )


def correct_kernel(
    plane, planes, x_ref, gain_ref, noise_hbm, weight_ref, pattern_ref, t1, t2, t3, flip, turn, out_ref,
    noise_ref, noise_sem, cube, cal, slab, part, from_left, from_right, land, fold,
    raw_send, raw_recv, right_send, right_recv, left_send, left_recv, back_send, back_recv,
):
    me = lax.axis_index("det")
    z, q = me // plane, me % plane
    dets, samples = x_ref.shape
    side = t1.shape[1]
    pairs = side // plane // 2
    rank = part.shape[1]
    lag = planes - 1
    mid_lag = max(lag + 1, 4)
    lead = min(3, pairs)
    noise_copy = pltpu.make_async_copy(noise_hbm, noise_ref, noise_sem)
    noise_copy.start()

    barrier = pltpu.get_barrier_semaphore()

    def partner(step):
        return lax.rem(q + step, plane)

    for step in range(1, plane):
        pl.semaphore_signal(barrier, inc=1, device_id={"det": z * plane + partner(step)})

    @pl.when(z > 0)
    def _():
        pl.semaphore_signal(barrier, inc=1, device_id={"det": me - plane})

    @pl.when(z < planes - 1)
    def _():
        pl.semaphore_signal(barrier, inc=1, device_id={"det": me + plane})

    def column(row):
        return pl.ds(pl.multiple_of(row * side, side), side)

    def slot(k):
        return pl.ds(pl.multiple_of(k * 2 * side, 2 * side), 2 * side)

    def spread(row):
        return pl.ds(row, dets, stride=side)

    def own_rows(owner):
        return pl.ds(pl.multiple_of(owner * dets, 8), dets)

    def raw_copy(pair, step):
        other = partner(step)
        return pltpu.make_async_remote_copy(
            src_ref=cal.at[:, slot(other * pairs + pair)],
            dst_ref=slab.at[pair, own_rows(q), :],
            send_sem=raw_send.at[pair, step - 1],
            recv_sem=raw_recv.at[pair, step - 1],
            device_id={"det": z * plane + other},
        )

    def back_copy(pair, step):
        other = partner(step)
        return pltpu.make_async_remote_copy(
            src_ref=slab.at[pair, own_rows(other), :],
            dst_ref=land.at[:, slot(q * pairs + pair)],
            send_sem=back_send.at[pair, step - 1],
            recv_sem=back_recv.at[pair, step - 1],
            device_id={"det": z * plane + other},
        )

    pieces = 4
    piece = [pl.ds(h * (rank // pieces), rank // pieces) for h in range(pieces)]

    def right_copy(pair, h):
        return pltpu.make_async_remote_copy(
            src_ref=from_left.at[pair, 1, piece[h], :],
            dst_ref=from_left.at[pair, 0, piece[h], :],
            send_sem=right_send.at[pair, h],
            recv_sem=right_recv.at[pair, h],
            device_id={"det": lax.rem(me + plane, plane * planes)},
        )

    def left_copy(pair, h):
        return pltpu.make_async_remote_copy(
            src_ref=from_right.at[pair, 1, piece[h], :],
            dst_ref=from_right.at[pair, 0, piece[h], :],
            send_sem=left_send.at[pair, h],
            recv_sem=left_recv.at[pair, h],
            device_id={"det": lax.rem(me + plane * (planes - 1), plane * planes)},
        )

    shape = (dets, dets)
    diagonal = lax.broadcasted_iota(jnp.int32, shape, 0) == lax.broadcasted_iota(jnp.int32, shape, 1)
    gain = jnp.sum(jnp.where(diagonal, gain_ref[...], 0.0), axis=1, keepdims=True)
    scale = jnp.broadcast_to(1.0 / gain, (dets, side))

    def to_cube(row, carry):
        cube[spread(row), :] = x_ref[:, column(row)] * scale
        return carry

    lax.fori_loop(0, side, to_cube, 0, unroll=8)
    first_table = (t1[0], t1[1])
    group = 8

    def first_stage(at, carry):
        rows = [pl.ds(pl.multiple_of((at * group + d) * side, side), side) for d in range(group)]
        section = product(first_table, split(jnp.concatenate([cube[row, :] for row in rows], axis=1)))
        for d in range(group):
            cube[rows[d], :] = section[:, d * side:(d + 1) * side]
        return carry

    lax.fori_loop(0, dets // group, first_stage, 0)
    at_ends = (z == 0).astype(jnp.int32) + (z == planes - 1).astype(jnp.int32)
    pl.semaphore_wait(barrier, plane + 1 - at_ends)

    def send_raw(pair, carry):
        for owner in range(plane):
            k = owner * pairs + pair
            cal[:, column(2 * k)] = cube[spread(2 * k), :]
            cal[:, column(2 * k + 1)] = cube[spread(2 * k + 1), :]
        for step in range(1, plane):
            raw_copy(pair, step).start()
        slab[pair, own_rows(q), :] = cal[:, slot(q * pairs + pair)]
        return carry

    lax.fori_loop(0, lead, send_raw, 0)
    in_plane = pl.ds(pl.multiple_of(z * plane * dets, 8), plane * dets)
    weight = split(weight_ref[in_plane, :].T)
    pattern = split(pattern_ref[in_plane, :])

    def measure_modes(pair):
        for step in range(1, plane):
            raw_copy(pair, step).wait_recv()
        part[pair] = product(weight, split(slab[pair]))

    measure_modes(0)

    def middle(real, imag, slots):
        turned = []
        for r, m, k in zip(real, imag, slots):
            cos, sin = turn[0, pl.ds(k, 1), :], turn[1, pl.ds(k, 1), :]
            turned.append(jnp.concatenate([r * cos + m * sin, m * cos - r * sin], axis=1))
        freq = product(split(jnp.concatenate(turned, axis=0)), (t2[0], t2[1]))
        weighted = []
        for at, k in enumerate(slots):
            noise = fold[own_rows(k), :]
            weighted.append(freq[at * dets:(at + 1) * dets] * jnp.concatenate([noise, noise], axis=1))
        section = product(split(jnp.concatenate(weighted, axis=0)), (t3[0], t3[1]))
        result = []
        for at, k in enumerate(slots):
            cos, sin = turn[0, pl.ds(k, 1), :], turn[1, pl.ds(k, 1), :]
            r, m = section[at * dets:(at + 1) * dets, :side], section[at * dets:(at + 1) * dets, side:]
            result.append((r * cos - m * sin, m * cos + r * sin))
        return result

    def one_step(i, carry):
        c_right = i - z
        c_left = i - (planes - 1 - z)

        def chain(h):
            rows = piece[h]

            @pl.when((c_right >= 0) & (c_right < pairs))
            def _():
                @pl.when(z == 0)
                def _():
                    from_left[c_right, 1, rows, :] = part[c_right, rows, :]

                @pl.when(z > 0)
                def _():
                    right_copy(c_right, h).wait_recv()
                    from_left[c_right, 1, rows, :] = part[c_right, rows, :] + from_left[c_right, 0, rows, :]

                @pl.when(z < planes - 1)
                def _():
                    right_copy(c_right, h).start()

            @pl.when((c_left >= 0) & (c_left < pairs))
            def _():
                @pl.when(z == planes - 1)
                def _():
                    from_right[c_left, 1, rows, :] = part[c_left, rows, :]

                @pl.when(z < planes - 1)
                def _():
                    left_copy(c_left, h).wait_recv()
                    from_right[c_left, 1, rows, :] = part[c_left, rows, :] + from_right[c_left, 0, rows, :]

                @pl.when(z > 0)
                def _():
                    left_copy(c_left, h).start()

        chain(0)

        @pl.when(i + 1 < pairs)
        def _():
            measure_modes(i + 1)

        @pl.when(i + lead < pairs)
        def _():
            send_raw(i + lead, 0)

        chain(1)

        @pl.when(i == 0)
        def _():
            noise_copy.wait()

        @pl.when(i < 2)
        def _():
            def regroup(at, carry):
                row = i * (side // 2) + at
                out_ref[spread(row), :] = noise_ref[:, column(row)]
                return carry

            lax.fori_loop(0, side // 2, regroup, 0, unroll=4)

        @pl.when((i >= 2) & (i < 4))
        def _():
            def swap(at, carry):
                det = (i - 2) * (dets // 2) + at
                fold[pl.ds(det, side, stride=dets), :] = out_ref[column(det), :].T
                return carry

            lax.fori_loop(0, dets // 2, swap, 0, unroll=2)

        @pl.when(i == 3)
        def _():
            def add_mirror(at, carry):
                ks = [1 + at * 3 + j for j in range(3)]
                high, low = split(jnp.concatenate([fold[own_rows(side - k), :] for k in ks], axis=0))
                dot = functools.partial(jnp.dot, preferred_element_type=jnp.float32)
                mirror = dot(high, flip[...]) + dot(low, flip[...])
                for j, k in enumerate(ks):
                    fold[own_rows(k), :] += mirror[j * dets:(j + 1) * dets]
                return carry

            lax.fori_loop(0, (side // 2 - 1) // 3, add_mirror, 0)

        chain(2)

        pair = i - mid_lag

        @pl.when((pair >= 0) & (pair < pairs))
        def _():
            for step in range(1, plane):
                back_copy(pair, step).wait_recv()
            slots = [owner * pairs + pair for owner in range(plane)]
            real = [land[:, column(2 * k)] for k in slots]
            imag = [land[:, column(2 * k + 1)] for k in slots]
            for k, (r, m) in zip(slots, middle(real, imag, slots)):
                out_ref[spread(2 * k), :] = r
                out_ref[spread(2 * k + 1), :] = m

            @pl.when(pair == 0)
            def _():
                none = jnp.zeros((dets, side), jnp.float32)
                ends = middle([real[0], imag[0]], [none, none], [0, side // 2])
                out_ref[spread(0), :] = ends[0][0]
                out_ref[spread(1), :] = ends[1][0]

        chain(3)
        c = i - lag

        @pl.when((c >= 0) & (c < pairs))
        def _():
            coeff = from_left[c, 1] + (from_right[c, 1] - part[c])
            slab[c] = slab[c] - product(pattern, split(coeff))
            for step in range(1, plane):
                back_copy(c, step).start()
            land[:, slot(q * pairs + c)] = slab[c, own_rows(q), :]

        return carry

    lax.fori_loop(0, pairs + mid_lag, one_step, 0)

    def finish(pair, carry):
        for step in range(1, plane):
            back_copy(pair, step).wait_send()
            raw_copy(pair, step).wait_send()

        @pl.when(z < planes - 1)
        def _():
            for h in range(pieces):
                right_copy(pair, h).wait_send()

        @pl.when(z > 0)
        def _():
            for h in range(pieces):
                left_copy(pair, h).wait_send()

        return carry

    lax.fori_loop(0, pairs, finish, 0)


def correct(stream, gains, noise, mode_pattern, mode_weights, tables, size):
    dets, samples = stream.shape
    rank = mode_pattern.shape[1]
    side = math.isqrt(samples)
    plane = 4 if size % 4 == 0 else 1
    planes = size // plane
    pairs = side // plane // 2
    rows = plane * dets
    f32 = jnp.float32
    vmem = pl.BlockSpec(memory_space=pltpu.VMEM)
    sem = pltpu.SemaphoreType.DMA
    coeffs = pltpu.VMEM((pairs, rank, 2 * side), f32)
    chain = pltpu.VMEM((pairs, 2, rank, 2 * side), f32)
    whole = pltpu.VMEM((dets, samples), f32)
    cube = pltpu.VMEM((dets * side, side), f32)
    return pl.pallas_call(
        functools.partial(correct_kernel, plane, planes),
        out_shape=jax.ShapeDtypeStruct((dets * side, side), f32),
        in_specs=[vmem, vmem, pl.BlockSpec(memory_space=pl.ANY)] + [vmem] * (2 + len(tables)),
        out_specs=pl.BlockSpec(memory_space=pltpu.VMEM),
        scratch_shapes=[
            whole, sem(()), cube, whole, pltpu.VMEM((pairs, rows, 2 * side), f32), coeffs, chain, chain, whole, cube,
            sem((pairs, plane)), sem((pairs, plane)), sem((pairs, 4)), sem((pairs, 4)),
            sem((pairs, 4)), sem((pairs, 4)), sem((pairs, plane)), sem((pairs, plane)),
        ],
        compiler_params=pltpu.CompilerParams(
            collective_id=0, has_side_effects=True, vmem_limit_bytes=60 * MIB
        ),
        name="correct",
    )(stream, gains, noise, mode_weights, mode_pattern, *tables)


def bin_kernel(x_ref, id_ref, hit_ref, sky_ref, t4, out_ref, acc_ref, count_ref, rows_ref, hits_ref):
    batch, side, _ = x_ref.shape
    per_row = PIX // side
    tiles = side // per_row
    packed = jnp.concatenate([x_ref[b] for b in range(batch)], axis=1)
    result = product((t4[0], t4[1]), split(packed))
    tiled = []
    for b in range(batch):
        part = result[:, b * side:(b + 1) * side]
        rows_ref[pl.ds(b * side, side), :] = part
        tiled.append(jnp.concatenate([part[p * tiles:(p + 1) * tiles] for p in range(per_row)], axis=1))
    for tile in range(tiles):
        for p in range(per_row):
            at = (tile * per_row + p) * side
            out_ref[:, at:at + side] = rows_ref[pl.ds(p * tiles + tile, batch, stride=side), :]
    high, low = split(jnp.concatenate(tiled, axis=0))
    blocks = acc_ref.shape[0]
    ladder = lax.broadcasted_iota(jnp.int32, (blocks, batch * tiles), 0)
    ids = jnp.concatenate([id_ref[b:b + 1, :] for b in range(batch)], axis=1)
    hits = jnp.concatenate([hit_ref[b:b + 1, :] for b in range(batch)], axis=1).astype(jnp.float32)
    table = jnp.where(ids == ladder, hits, 0.0)
    counts = table[:, :LANES]
    for at in range(LANES, batch * tiles, LANES):
        counts = counts + table[:, at:at + LANES]
    table = table.astype(jnp.bfloat16)
    dot = functools.partial(jnp.dot, preferred_element_type=jnp.float32)

    @pl.when(pl.program_id(0) == 0)
    def _():
        acc_ref[...] = jnp.zeros_like(acc_ref)
        hits_ref[...] = jnp.zeros_like(hits_ref)

    acc_ref[...] += dot(table, high) + dot(table, low)
    hits_ref[...] += counts

    @pl.when(pl.program_id(0) == pl.num_programs(0) - 1)
    def _():
        ladder = lax.broadcasted_iota(jnp.int32, (blocks, blocks), 0)
        place = jnp.where(sky_ref[...] == ladder, 1.0, 0.0).astype(jnp.bfloat16)
        total = acc_ref[...]
        high, low = split(total)
        rest = (total - high.astype(jnp.float32) - low.astype(jnp.float32)).astype(jnp.bfloat16)
        acc_ref[...] = dot(place, high) + (dot(place, low) + dot(place, rest))
        high, low = split(hits_ref[...])
        tally = split(dot(place, high) + dot(place, low))
        ones = jnp.ones((8, LANES), jnp.bfloat16)
        across = functools.partial(
            lax.dot_general, dimension_numbers=(((1,), (1,)), ((), ())), preferred_element_type=jnp.float32
        )
        count_ref[...] = (across(ones, tally[0]) + across(ones, tally[1]))[:1]


def finish_and_bin(packed, ids, hits, sky_rows, table):
    dets, side, _ = packed.shape
    batch = 16 if dets % 16 == 0 else 8
    tiles = side * side // PIX
    blocks = sky_rows.shape[1]
    line = pl.BlockSpec((batch, tiles), lambda i: (i, 0))
    return pl.pallas_call(
        bin_kernel,
        grid=(dets // batch,),
        out_shape=(
            jax.ShapeDtypeStruct((dets, side * side), jnp.float32),
            jax.ShapeDtypeStruct((blocks, PIX), jnp.float32),
            jax.ShapeDtypeStruct((1, blocks), jnp.float32),
        ),
        in_specs=[
            pl.BlockSpec((batch, side, side), lambda i: (i, 0, 0)),
            line,
            line,
            pl.BlockSpec((1, blocks), lambda i: (0, 0)),
            pl.BlockSpec(table.shape, lambda i: (0, 0, 0)),
        ],
        out_specs=(
            pl.BlockSpec((batch, side * side), lambda i: (i, 0)),
            pl.BlockSpec((blocks, PIX), lambda i: (0, 0)),
            pl.BlockSpec((1, blocks), lambda i: (0, 0)),
        ),
        scratch_shapes=[pltpu.VMEM((batch * side, side), jnp.float32), pltpu.VMEM((blocks, LANES), jnp.float32)],
        compiler_params=pltpu.CompilerParams(vmem_limit_bytes=60 * MIB),
        name="finish_and_bin",
    )(packed, ids, hits, sky_rows, table)


def map_kernel(
    plane, planes, acc_ref, count_ref, out_ref,
    near, near_tally, partial, tally, far, far_tally,
    near_send, near_recv, near_tally_send, near_tally_recv, far_send, far_recv, far_tally_send, far_tally_recv,
):
    me = lax.axis_index("det")
    z, q = me // plane, me % plane
    rows, columns = out_ref.shape
    barrier = pltpu.get_barrier_semaphore()

    def neighbour(step):
        return z * plane + lax.rem(q + step, plane)

    def beyond(step):
        return lax.rem(me + step * plane, plane * planes)

    for step in range(1, plane):
        pl.semaphore_signal(barrier, inc=1, device_id={"det": neighbour(step)})
    for step in range(1, planes):
        pl.semaphore_signal(barrier, inc=1, device_id={"det": beyond(step)})
    pl.semaphore_wait(barrier, plane + planes - 2)

    def share(owner):
        return pl.ds(pl.multiple_of(owner * rows, 8), rows)

    def remote(source, target, send_sem, recv_sem, device):
        return pltpu.make_async_remote_copy(
            src_ref=source, dst_ref=target, send_sem=send_sem, recv_sem=recv_sem, device_id={"det": device}
        )

    first, second = [], []
    for step in range(1, plane):
        source = acc_ref.at[:, share(lax.rem(q + step, plane)), :]
        at = step - 1
        first.append((
            remote(source, near.at[at], near_send.at[at], near_recv.at[at], neighbour(step)),
            remote(count_ref, near_tally.at[at], near_tally_send.at[at], near_tally_recv.at[at], neighbour(step)),
        ))
    for step in range(1, planes):
        at = step - 1
        source = partial.at[lax.rem(z + step, planes)]
        second.append((
            remote(source, far.at[at], far_send.at[at], far_recv.at[at], beyond(step)),
            remote(tally, far_tally.at[at], far_tally_send.at[at], far_tally_recv.at[at], beyond(step)),
        ))
    for pair in first:
        for copy in pair:
            copy.start()
    sums, counts = acc_ref[:, share(q), :], count_ref[...]
    for at, pair in enumerate(first):
        for copy in pair:
            copy.wait_recv()
        sums, counts = sums + near[at], counts + near_tally[at]
    partial[...] = sums
    tally[...] = counts
    for pair in second:
        for copy in pair:
            copy.start()
    sums = partial[z]
    for at, pair in enumerate(second):
        for copy in pair:
            copy.wait_recv()
        sums, counts = sums + far[at], counts + far_tally[at]
    shape = (rows, counts.shape[1])
    mine = lax.broadcasted_iota(jnp.int32, shape, 1) == lax.broadcasted_iota(jnp.int32, shape, 0) + me * rows
    counts = jnp.sum(jnp.where(mine, counts, 0.0), axis=1, keepdims=True)
    out_ref[...] = sums / jnp.sqrt(1.0 + counts)
    for pair in first + second:
        for copy in pair:
            copy.wait_send()


def combine_map(acc, counts, size):
    blocks, columns = acc.shape
    rows = blocks // size
    plane = 4 if size % 4 == 0 else 1
    planes = size // plane
    near, far = max(1, plane - 1), max(1, planes - 1)
    sems = [pltpu.SemaphoreType.DMA((near,))] * 4 + [pltpu.SemaphoreType.DMA((far,))] * 4
    f32 = jnp.float32
    return pl.pallas_call(
        functools.partial(map_kernel, plane, planes),
        out_shape=jax.ShapeDtypeStruct((rows, columns), f32),
        in_specs=[pl.BlockSpec(memory_space=pltpu.VMEM)] * 2,
        out_specs=pl.BlockSpec(memory_space=pltpu.VMEM),
        scratch_shapes=[
            pltpu.VMEM((near, planes, rows, columns), f32),
            pltpu.VMEM((near, 1, blocks), f32),
            pltpu.VMEM((planes, rows, columns), f32),
            pltpu.VMEM((1, blocks), f32),
            pltpu.VMEM((far, rows, columns), f32),
            pltpu.VMEM((far, 1, blocks), f32),
            *sems,
        ],
        compiler_params=pltpu.CompilerParams(collective_id=1, has_side_effects=True),
        name="combine_map",
    )(acc.reshape(planes, plane * rows, columns), counts)


def shards(size, timestream, gains, mode_pattern, mode_weights, noise_weight, block_ids, hits, sky_rows):
    items, dets, samples = timestream.shape
    side = math.isqrt(samples)
    *tables, last = [jnp.asarray(table) for table in transform_tables(side)]
    packed = correct(
        timestream.reshape(items * dets, samples), gains, noise_weight, mode_pattern, mode_weights,
        tables, size,
    )
    filtered, acc, counts = finish_and_bin(
        packed.reshape(dets, side, side), block_ids.reshape(dets, -1), hits.reshape(dets, -1), sky_rows[None, :], last
    )
    return (filtered.reshape(items, dets, samples), combine_map(acc, counts, size))


def solution(mesh):
    in_specs = (
        P("grp", "det", None),
        P("grp", "det"),
        P("grp", None),
        P("grp", None),
        P(("grp", "det"), None),
        P("grp", "det", None),
        P("grp", "det", None),
        P("grp"),
    )
    out_specs = (P("grp", "det", None), P(("grp", "det"), None))
    body = functools.partial(shards, mesh.shape["det"])
    return jax.shard_map(body, mesh=mesh, in_specs=in_specs, out_specs=out_specs, check_vma=False)
```

```python
import functools
import math

import jax
import jax.numpy as jnp
import ml_dtypes
import numpy as np
from jax import lax
from jax.experimental import pallas as pl
from jax.experimental.pallas import tpu as pltpu
from jax.sharding import PartitionSpec as P

PIX = 256
LANES = 128
MIB = 1 << 20


def split(value):
    high = value.astype(jnp.bfloat16)
    return high, (value - high.astype(jnp.float32)).astype(jnp.bfloat16)


def product(left, right):
    high, low = left
    left = jnp.concatenate([high, high, low], axis=1)
    high, low = right
    right = jnp.concatenate([high, low, high], axis=0)
    return jnp.dot(left, right, preferred_element_type=jnp.float32)


def halves(table):
    high = table.astype(ml_dtypes.bfloat16)
    low = (table - high.astype(np.float64)).astype(ml_dtypes.bfloat16)
    return np.stack([high, low])


def transform_tables(side):
    index = np.arange(side)
    angle = (np.outer(index, index) % side) * (2.0 * math.pi / side)
    cos, sin = np.cos(angle), np.sin(angle)
    packed = np.stack([cos[: side // 2], -sin[: side // 2]], 1).reshape(side, side)
    packed[1] = cos[side // 2]
    twist = np.outer(np.arange(side // 2 + 1), index) * (2.0 * math.pi / (side * side))
    turn = np.stack([np.cos(twist), np.sin(twist)]).astype(np.float32)
    per_row = PIX // side
    last = packed.T / (side * side)
    last = last.reshape(side // per_row, per_row, side).swapaxes(0, 1).reshape(side, side)
    return (
        halves(packed),
        halves(np.block([[cos, -sin], [sin, cos]])),
        halves(np.block([[cos, sin], [-sin, cos]])),
        np.eye(side)[::-1].astype(ml_dtypes.bfloat16),
        turn,
        halves(last),
    )


def correct_kernel(
    plane, planes, x_ref, gain_ref, noise_hbm, weight_ref, pattern_ref, t1, t2, t3, flip, turn, out_ref,
    noise_ref, noise_sem, cube, cal, slab, part, from_left, from_right, land, fold,
    raw_send, raw_recv, right_send, right_recv, left_send, left_recv, back_send, back_recv,
):
    me = lax.axis_index("det")
    z, q = me // plane, me % plane
    dets, samples = x_ref.shape
    side = t1.shape[1]
    pairs = side // plane // 2
    rank = part.shape[1]
    lag = planes - 1
    mid_lag = max(lag + 1, 4)
    lead = min(3, pairs)
    noise_copy = pltpu.make_async_copy(noise_hbm, noise_ref, noise_sem)
    noise_copy.start()

    barrier = pltpu.get_barrier_semaphore()

    def partner(step):
        return lax.rem(q + step, plane)

    for step in range(1, plane):
        pl.semaphore_signal(barrier, inc=1, device_id={"det": z * plane + partner(step)})

    @pl.when(z > 0)
    def _():
        pl.semaphore_signal(barrier, inc=1, device_id={"det": me - plane})

    @pl.when(z < planes - 1)
    def _():
        pl.semaphore_signal(barrier, inc=1, device_id={"det": me + plane})

    def column(row):
        return pl.ds(pl.multiple_of(row * side, side), side)

    def slot(k):
        return pl.ds(pl.multiple_of(k * 2 * side, 2 * side), 2 * side)

    def spread(row):
        return pl.ds(row, dets, stride=side)

    def own_rows(owner):
        return pl.ds(pl.multiple_of(owner * dets, 8), dets)

    def raw_copy(pair, step):
        other = partner(step)
        return pltpu.make_async_remote_copy(
            src_ref=cal.at[:, slot(other * pairs + pair)],
            dst_ref=slab.at[pair, own_rows(q), :],
            send_sem=raw_send.at[pair, step - 1],
            recv_sem=raw_recv.at[pair, step - 1],
            device_id={"det": z * plane + other},
        )

    def back_copy(pair, step):
        other = partner(step)
        return pltpu.make_async_remote_copy(
            src_ref=slab.at[pair, own_rows(other), :],
            dst_ref=land.at[:, slot(q * pairs + pair)],
            send_sem=back_send.at[pair, step - 1],
            recv_sem=back_recv.at[pair, step - 1],
            device_id={"det": z * plane + other},
        )

    halves_of = [pl.ds(h * (rank // 2), rank // 2) for h in range(2)]

    def right_copy(pair, h):
        return pltpu.make_async_remote_copy(
            src_ref=from_left.at[pair, 1, halves_of[h], :],
            dst_ref=from_left.at[pair, 0, halves_of[h], :],
            send_sem=right_send.at[pair, h],
            recv_sem=right_recv.at[pair, h],
            device_id={"det": lax.rem(me + plane, plane * planes)},
        )

    def left_copy(pair, h):
        return pltpu.make_async_remote_copy(
            src_ref=from_right.at[pair, 1, halves_of[h], :],
            dst_ref=from_right.at[pair, 0, halves_of[h], :],
            send_sem=left_send.at[pair, h],
            recv_sem=left_recv.at[pair, h],
            device_id={"det": lax.rem(me + plane * (planes - 1), plane * planes)},
        )

    shape = (dets, dets)
    diagonal = lax.broadcasted_iota(jnp.int32, shape, 0) == lax.broadcasted_iota(jnp.int32, shape, 1)
    gain = jnp.sum(jnp.where(diagonal, gain_ref[...], 0.0), axis=1, keepdims=True)
    scale = jnp.broadcast_to(1.0 / gain, (dets, side))

    def to_cube(row, carry):
        cube[spread(row), :] = x_ref[:, column(row)] * scale
        return carry

    lax.fori_loop(0, side, to_cube, 0, unroll=8)
    first_table = (t1[0], t1[1])
    group = 8

    def first_stage(at, carry):
        rows = [pl.ds(pl.multiple_of((at * group + d) * side, side), side) for d in range(group)]
        section = product(first_table, split(jnp.concatenate([cube[row, :] for row in rows], axis=1)))
        for d in range(group):
            cube[rows[d], :] = section[:, d * side:(d + 1) * side]
        return carry

    lax.fori_loop(0, dets // group, first_stage, 0)
    at_ends = (z == 0).astype(jnp.int32) + (z == planes - 1).astype(jnp.int32)
    pl.semaphore_wait(barrier, plane + 1 - at_ends)

    def send_raw(pair, carry):
        for owner in range(plane):
            k = owner * pairs + pair
            cal[:, column(2 * k)] = cube[spread(2 * k), :]
            cal[:, column(2 * k + 1)] = cube[spread(2 * k + 1), :]
        for step in range(1, plane):
            raw_copy(pair, step).start()
        slab[pair, own_rows(q), :] = cal[:, slot(q * pairs + pair)]
        return carry

    lax.fori_loop(0, lead, send_raw, 0)
    in_plane = pl.ds(pl.multiple_of(z * plane * dets, 8), plane * dets)
    weight = split(weight_ref[in_plane, :].T)
    pattern = split(pattern_ref[in_plane, :])

    def measure_modes(pair):
        for step in range(1, plane):
            raw_copy(pair, step).wait_recv()
        part[pair] = product(weight, split(slab[pair]))

    measure_modes(0)

    def middle(real, imag, slots):
        turned = []
        for r, m, k in zip(real, imag, slots):
            cos, sin = turn[0, pl.ds(k, 1), :], turn[1, pl.ds(k, 1), :]
            turned.append(jnp.concatenate([r * cos + m * sin, m * cos - r * sin], axis=1))
        freq = product(split(jnp.concatenate(turned, axis=0)), (t2[0], t2[1]))
        weighted = []
        for at, k in enumerate(slots):
            noise = fold[own_rows(k), :]
            weighted.append(freq[at * dets:(at + 1) * dets] * jnp.concatenate([noise, noise], axis=1))
        section = product(split(jnp.concatenate(weighted, axis=0)), (t3[0], t3[1]))
        result = []
        for at, k in enumerate(slots):
            cos, sin = turn[0, pl.ds(k, 1), :], turn[1, pl.ds(k, 1), :]
            r, m = section[at * dets:(at + 1) * dets, :side], section[at * dets:(at + 1) * dets, side:]
            result.append((r * cos - m * sin, m * cos + r * sin))
        return result

    def one_step(i, carry):
        c_right = i - z
        c_left = i - (planes - 1 - z)
        for h in range(2):
            rows = halves_of[h]

            @pl.when((c_right >= 0) & (c_right < pairs))
            def _():
                @pl.when(z == 0)
                def _():
                    from_left[c_right, 1, rows, :] = part[c_right, rows, :]

                @pl.when(z > 0)
                def _():
                    right_copy(c_right, h).wait_recv()
                    from_left[c_right, 1, rows, :] = part[c_right, rows, :] + from_left[c_right, 0, rows, :]

                @pl.when(z < planes - 1)
                def _():
                    right_copy(c_right, h).start()

            @pl.when((c_left >= 0) & (c_left < pairs))
            def _():
                @pl.when(z == planes - 1)
                def _():
                    from_right[c_left, 1, rows, :] = part[c_left, rows, :]

                @pl.when(z < planes - 1)
                def _():
                    left_copy(c_left, h).wait_recv()
                    from_right[c_left, 1, rows, :] = part[c_left, rows, :] + from_right[c_left, 0, rows, :]

                @pl.when(z > 0)
                def _():
                    left_copy(c_left, h).start()

        @pl.when(i + lead < pairs)
        def _():
            send_raw(i + lead, 0)

        c = i - lag

        @pl.when((c >= 0) & (c < pairs))
        def _():
            coeff = from_left[c, 1] + (from_right[c, 1] - part[c])
            slab[c] = slab[c] - product(pattern, split(coeff))
            for step in range(1, plane):
                back_copy(c, step).start()
            land[:, slot(q * pairs + c)] = slab[c, own_rows(q), :]

        @pl.when(i + 1 < pairs)
        def _():
            measure_modes(i + 1)

        @pl.when(i == 0)
        def _():
            noise_copy.wait()

        @pl.when(i < 2)
        def _():
            def regroup(at, carry):
                row = i * (side // 2) + at
                out_ref[spread(row), :] = noise_ref[:, column(row)]
                return carry

            lax.fori_loop(0, side // 2, regroup, 0, unroll=4)

        @pl.when((i >= 2) & (i < 4))
        def _():
            def swap(at, carry):
                det = (i - 2) * (dets // 2) + at
                fold[pl.ds(det, side, stride=dets), :] = out_ref[column(det), :].T
                return carry

            lax.fori_loop(0, dets // 2, swap, 0, unroll=2)

        @pl.when(i == 3)
        def _():
            def add_mirror(at, carry):
                ks = [1 + at * 3 + j for j in range(3)]
                high, low = split(jnp.concatenate([fold[own_rows(side - k), :] for k in ks], axis=0))
                dot = functools.partial(jnp.dot, preferred_element_type=jnp.float32)
                mirror = dot(high, flip[...]) + dot(low, flip[...])
                for j, k in enumerate(ks):
                    fold[own_rows(k), :] += mirror[j * dets:(j + 1) * dets]
                return carry

            lax.fori_loop(0, (side // 2 - 1) // 3, add_mirror, 0)

        pair = i - mid_lag

        @pl.when((pair >= 0) & (pair < pairs))
        def _():
            for step in range(1, plane):
                back_copy(pair, step).wait_recv()
            slots = [owner * pairs + pair for owner in range(plane)]
            real = [land[:, column(2 * k)] for k in slots]
            imag = [land[:, column(2 * k + 1)] for k in slots]
            for k, (r, m) in zip(slots, middle(real, imag, slots)):
                out_ref[spread(2 * k), :] = r
                out_ref[spread(2 * k + 1), :] = m

            @pl.when(pair == 0)
            def _():
                none = jnp.zeros((dets, side), jnp.float32)
                ends = middle([real[0], imag[0]], [none, none], [0, side // 2])
                out_ref[spread(0), :] = ends[0][0]
                out_ref[spread(1), :] = ends[1][0]

        return carry

    lax.fori_loop(0, pairs + mid_lag, one_step, 0)

    def finish(pair, carry):
        for step in range(1, plane):
            back_copy(pair, step).wait_send()
            raw_copy(pair, step).wait_send()

        @pl.when(z < planes - 1)
        def _():
            for h in range(2):
                right_copy(pair, h).wait_send()

        @pl.when(z > 0)
        def _():
            for h in range(2):
                left_copy(pair, h).wait_send()

        return carry

    lax.fori_loop(0, pairs, finish, 0)


def correct(stream, gains, noise, mode_pattern, mode_weights, tables, size):
    dets, samples = stream.shape
    rank = mode_pattern.shape[1]
    side = math.isqrt(samples)
    plane = 4 if size % 4 == 0 else 1
    planes = size // plane
    pairs = side // plane // 2
    rows = plane * dets
    f32 = jnp.float32
    vmem = pl.BlockSpec(memory_space=pltpu.VMEM)
    sem = pltpu.SemaphoreType.DMA
    coeffs = pltpu.VMEM((pairs, rank, 2 * side), f32)
    chain = pltpu.VMEM((pairs, 2, rank, 2 * side), f32)
    whole = pltpu.VMEM((dets, samples), f32)
    cube = pltpu.VMEM((dets * side, side), f32)
    return pl.pallas_call(
        functools.partial(correct_kernel, plane, planes),
        out_shape=jax.ShapeDtypeStruct((dets * side, side), f32),
        in_specs=[vmem, vmem, pl.BlockSpec(memory_space=pl.ANY)] + [vmem] * (2 + len(tables)),
        out_specs=pl.BlockSpec(memory_space=pltpu.VMEM),
        scratch_shapes=[
            whole, sem(()), cube, whole, pltpu.VMEM((pairs, rows, 2 * side), f32), coeffs, chain, chain, whole, cube,
            sem((pairs, plane)), sem((pairs, plane)), sem((pairs, 2)), sem((pairs, 2)),
            sem((pairs, 2)), sem((pairs, 2)), sem((pairs, plane)), sem((pairs, plane)),
        ],
        compiler_params=pltpu.CompilerParams(
            collective_id=0, has_side_effects=True, vmem_limit_bytes=60 * MIB
        ),
        name="correct",
    )(stream, gains, noise, mode_weights, mode_pattern, *tables)


def bin_kernel(x_ref, id_ref, hit_ref, sky_ref, t4, out_ref, acc_ref, count_ref, rows_ref, hits_ref):
    batch, side, _ = x_ref.shape
    per_row = PIX // side
    tiles = side // per_row
    packed = jnp.concatenate([x_ref[b] for b in range(batch)], axis=1)
    result = product((t4[0], t4[1]), split(packed))
    tiled = []
    for b in range(batch):
        part = result[:, b * side:(b + 1) * side]
        rows_ref[pl.ds(b * side, side), :] = part
        tiled.append(jnp.concatenate([part[p * tiles:(p + 1) * tiles] for p in range(per_row)], axis=1))
    for tile in range(tiles):
        for p in range(per_row):
            at = (tile * per_row + p) * side
            out_ref[:, at:at + side] = rows_ref[pl.ds(p * tiles + tile, batch, stride=side), :]
    high, low = split(jnp.concatenate(tiled, axis=0))
    blocks = acc_ref.shape[0]
    ladder = lax.broadcasted_iota(jnp.int32, (blocks, batch * tiles), 0)
    ids = jnp.concatenate([id_ref[b:b + 1, :] for b in range(batch)], axis=1)
    hits = jnp.concatenate([hit_ref[b:b + 1, :] for b in range(batch)], axis=1).astype(jnp.float32)
    table = jnp.where(ids == ladder, hits, 0.0)
    counts = table[:, :LANES]
    for at in range(LANES, batch * tiles, LANES):
        counts = counts + table[:, at:at + LANES]
    table = table.astype(jnp.bfloat16)
    dot = functools.partial(jnp.dot, preferred_element_type=jnp.float32)

    @pl.when(pl.program_id(0) == 0)
    def _():
        acc_ref[...] = jnp.zeros_like(acc_ref)
        hits_ref[...] = jnp.zeros_like(hits_ref)

    acc_ref[...] += dot(table, high) + dot(table, low)
    hits_ref[...] += counts

    @pl.when(pl.program_id(0) == pl.num_programs(0) - 1)
    def _():
        ladder = lax.broadcasted_iota(jnp.int32, (blocks, blocks), 0)
        place = jnp.where(sky_ref[...] == ladder, 1.0, 0.0).astype(jnp.bfloat16)
        total = acc_ref[...]
        high, low = split(total)
        rest = (total - high.astype(jnp.float32) - low.astype(jnp.float32)).astype(jnp.bfloat16)
        acc_ref[...] = dot(place, high) + (dot(place, low) + dot(place, rest))
        high, low = split(hits_ref[...])
        tally = split(dot(place, high) + dot(place, low))
        ones = jnp.ones((8, LANES), jnp.bfloat16)
        across = functools.partial(
            lax.dot_general, dimension_numbers=(((1,), (1,)), ((), ())), preferred_element_type=jnp.float32
        )
        count_ref[...] = (across(ones, tally[0]) + across(ones, tally[1]))[:1]


def finish_and_bin(packed, ids, hits, sky_rows, table):
    dets, side, _ = packed.shape
    batch = 16 if dets % 16 == 0 else 8
    tiles = side * side // PIX
    blocks = sky_rows.shape[1]
    line = pl.BlockSpec((batch, tiles), lambda i: (i, 0))
    return pl.pallas_call(
        bin_kernel,
        grid=(dets // batch,),
        out_shape=(
            jax.ShapeDtypeStruct((dets, side * side), jnp.float32),
            jax.ShapeDtypeStruct((blocks, PIX), jnp.float32),
            jax.ShapeDtypeStruct((1, blocks), jnp.float32),
        ),
        in_specs=[
            pl.BlockSpec((batch, side, side), lambda i: (i, 0, 0)),
            line,
            line,
            pl.BlockSpec((1, blocks), lambda i: (0, 0)),
            pl.BlockSpec(table.shape, lambda i: (0, 0, 0)),
        ],
        out_specs=(
            pl.BlockSpec((batch, side * side), lambda i: (i, 0)),
            pl.BlockSpec((blocks, PIX), lambda i: (0, 0)),
            pl.BlockSpec((1, blocks), lambda i: (0, 0)),
        ),
        scratch_shapes=[pltpu.VMEM((batch * side, side), jnp.float32), pltpu.VMEM((blocks, LANES), jnp.float32)],
        compiler_params=pltpu.CompilerParams(vmem_limit_bytes=60 * MIB),
        name="finish_and_bin",
    )(packed, ids, hits, sky_rows, table)


def map_kernel(
    plane, planes, acc_ref, count_ref, out_ref,
    near, near_tally, partial, tally, far, far_tally,
    near_send, near_recv, near_tally_send, near_tally_recv, far_send, far_recv, far_tally_send, far_tally_recv,
):
    me = lax.axis_index("det")
    z, q = me // plane, me % plane
    rows, columns = out_ref.shape
    barrier = pltpu.get_barrier_semaphore()

    def neighbour(step):
        return z * plane + lax.rem(q + step, plane)

    def beyond(step):
        return lax.rem(me + step * plane, plane * planes)

    for step in range(1, plane):
        pl.semaphore_signal(barrier, inc=1, device_id={"det": neighbour(step)})
    for step in range(1, planes):
        pl.semaphore_signal(barrier, inc=1, device_id={"det": beyond(step)})
    pl.semaphore_wait(barrier, plane + planes - 2)

    def share(owner):
        return pl.ds(pl.multiple_of(owner * rows, 8), rows)

    def remote(source, target, send_sem, recv_sem, device):
        return pltpu.make_async_remote_copy(
            src_ref=source, dst_ref=target, send_sem=send_sem, recv_sem=recv_sem, device_id={"det": device}
        )

    first, second = [], []
    for step in range(1, plane):
        source = acc_ref.at[:, share(lax.rem(q + step, plane)), :]
        at = step - 1
        first.append((
            remote(source, near.at[at], near_send.at[at], near_recv.at[at], neighbour(step)),
            remote(count_ref, near_tally.at[at], near_tally_send.at[at], near_tally_recv.at[at], neighbour(step)),
        ))
    for step in range(1, planes):
        at = step - 1
        source = partial.at[lax.rem(z + step, planes)]
        second.append((
            remote(source, far.at[at], far_send.at[at], far_recv.at[at], beyond(step)),
            remote(tally, far_tally.at[at], far_tally_send.at[at], far_tally_recv.at[at], beyond(step)),
        ))
    for pair in first:
        for copy in pair:
            copy.start()
    sums, counts = acc_ref[:, share(q), :], count_ref[...]
    for at, pair in enumerate(first):
        for copy in pair:
            copy.wait_recv()
        sums, counts = sums + near[at], counts + near_tally[at]
    partial[...] = sums
    tally[...] = counts
    for pair in second:
        for copy in pair:
            copy.start()
    sums = partial[z]
    for at, pair in enumerate(second):
        for copy in pair:
            copy.wait_recv()
        sums, counts = sums + far[at], counts + far_tally[at]
    shape = (rows, counts.shape[1])
    mine = lax.broadcasted_iota(jnp.int32, shape, 1) == lax.broadcasted_iota(jnp.int32, shape, 0) + me * rows
    counts = jnp.sum(jnp.where(mine, counts, 0.0), axis=1, keepdims=True)
    out_ref[...] = sums / jnp.sqrt(1.0 + counts)
    for pair in first + second:
        for copy in pair:
            copy.wait_send()


def combine_map(acc, counts, size):
    blocks, columns = acc.shape
    rows = blocks // size
    plane = 4 if size % 4 == 0 else 1
    planes = size // plane
    near, far = max(1, plane - 1), max(1, planes - 1)
    sems = [pltpu.SemaphoreType.DMA((near,))] * 4 + [pltpu.SemaphoreType.DMA((far,))] * 4
    f32 = jnp.float32
    return pl.pallas_call(
        functools.partial(map_kernel, plane, planes),
        out_shape=jax.ShapeDtypeStruct((rows, columns), f32),
        in_specs=[pl.BlockSpec(memory_space=pltpu.VMEM)] * 2,
        out_specs=pl.BlockSpec(memory_space=pltpu.VMEM),
        scratch_shapes=[
            pltpu.VMEM((near, planes, rows, columns), f32),
            pltpu.VMEM((near, 1, blocks), f32),
            pltpu.VMEM((planes, rows, columns), f32),
            pltpu.VMEM((1, blocks), f32),
            pltpu.VMEM((far, rows, columns), f32),
            pltpu.VMEM((far, 1, blocks), f32),
            *sems,
        ],
        compiler_params=pltpu.CompilerParams(collective_id=1, has_side_effects=True),
        name="combine_map",
    )(acc.reshape(planes, plane * rows, columns), counts)


def shards(size, timestream, gains, mode_pattern, mode_weights, noise_weight, block_ids, hits, sky_rows):
    items, dets, samples = timestream.shape
    side = math.isqrt(samples)
    *tables, last = [jnp.asarray(table) for table in transform_tables(side)]
    packed = correct(
        timestream.reshape(items * dets, samples), gains, noise_weight, mode_pattern, mode_weights,
        tables, size,
    )
    filtered, acc, counts = finish_and_bin(
        packed.reshape(dets, side, side), block_ids.reshape(dets, -1), hits.reshape(dets, -1), sky_rows[None, :], last
    )
    return (filtered.reshape(items, dets, samples), combine_map(acc, counts, size))


def solution(mesh):
    in_specs = (
        P("grp", "det", None),
        P("grp", "det"),
        P("grp", None),
        P("grp", None),
        P(("grp", "det"), None),
        P("grp", "det", None),
        P("grp", "det", None),
        P("grp"),
    )
    out_specs = (P("grp", "det", None), P(("grp", "det"), None))
    body = functools.partial(shards, mesh.shape["det"])
    return jax.shard_map(body, mesh=mesh, in_specs=in_specs, out_specs=out_specs, check_vma=False)
```

```python
import functools
import math

import jax
import jax.numpy as jnp
import ml_dtypes
import numpy as np
from jax import lax
from jax.experimental import pallas as pl
from jax.experimental.pallas import tpu as pltpu
from jax.sharding import PartitionSpec as P

PIX = 256
LANES = 128
MIB = 1 << 20


def split(value):
    high = value.astype(jnp.bfloat16)
    return high, (value - high.astype(jnp.float32)).astype(jnp.bfloat16)


def product(left, right):
    high, low = left
    left = jnp.concatenate([high, high, low], axis=1)
    high, low = right
    right = jnp.concatenate([high, low, high], axis=0)
    return jnp.dot(left, right, preferred_element_type=jnp.float32)


def halves(table):
    high = table.astype(ml_dtypes.bfloat16)
    low = (table - high.astype(np.float64)).astype(ml_dtypes.bfloat16)
    return np.stack([high, low])


def transform_tables(side):
    index = np.arange(side)
    angle = (np.outer(index, index) % side) * (2.0 * math.pi / side)
    cos, sin = np.cos(angle), np.sin(angle)
    packed = np.stack([cos[: side // 2], -sin[: side // 2]], 1).reshape(side, side)
    packed[1] = cos[side // 2]
    twist = np.outer(np.arange(side // 2 + 1), index) * (2.0 * math.pi / (side * side))
    turn = np.stack([np.cos(twist), np.sin(twist)]).astype(np.float32)
    per_row = PIX // side
    last = packed.T / (side * side)
    last = last.reshape(side // per_row, per_row, side).swapaxes(0, 1).reshape(side, side)
    return (
        halves(packed),
        halves(np.block([[cos, -sin], [sin, cos]])),
        halves(np.block([[cos, sin], [-sin, cos]])),
        np.eye(side)[::-1].astype(ml_dtypes.bfloat16),
        turn,
        halves(last),
    )


def correct_kernel(
    plane, planes, x_ref, gain_ref, noise_hbm, weight_ref, pattern_ref, t1, t2, t3, flip, turn, out_ref,
    noise_ref, noise_sem, cube, cal, slab, part, from_left, from_right, land, fold,
    raw_send, raw_recv, right_send, right_recv, left_send, left_recv, back_send, back_recv,
):
    me = lax.axis_index("det")
    z, q = me // plane, me % plane
    dets, samples = x_ref.shape
    side = t1.shape[1]
    pairs = side // plane // 2
    rank = part.shape[1]
    lag = planes - 1
    ready = 8
    mid_lag = lag + 1
    assert mid_lag >= ready or (mid_lag == ready // 2 and pairs >= ready)
    lead = min(3, pairs)
    noise_copy = pltpu.make_async_copy(noise_hbm, noise_ref, noise_sem)
    noise_copy.start()

    barrier = pltpu.get_barrier_semaphore()

    def partner(step):
        return lax.rem(q + step, plane)

    for step in range(1, plane):
        pl.semaphore_signal(barrier, inc=1, device_id={"det": z * plane + partner(step)})

    @pl.when(z > 0)
    def _():
        pl.semaphore_signal(barrier, inc=1, device_id={"det": me - plane})

    @pl.when(z < planes - 1)
    def _():
        pl.semaphore_signal(barrier, inc=1, device_id={"det": me + plane})

    def column(row):
        return pl.ds(pl.multiple_of(row * side, side), side)

    def slot(k):
        return pl.ds(pl.multiple_of(k * 2 * side, 2 * side), 2 * side)

    def spread(row):
        return pl.ds(row, dets, stride=side)

    def own_rows(owner):
        return pl.ds(pl.multiple_of(owner * dets, 8), dets)

    def raw_copy(pair, step):
        other = partner(step)
        return pltpu.make_async_remote_copy(
            src_ref=cal.at[:, slot(other * pairs + pair)],
            dst_ref=slab.at[pair, own_rows(q), :],
            send_sem=raw_send.at[pair, step - 1],
            recv_sem=raw_recv.at[pair, step - 1],
            device_id={"det": z * plane + other},
        )

    def back_copy(pair, step):
        other = partner(step)
        return pltpu.make_async_remote_copy(
            src_ref=slab.at[pair, own_rows(other), :],
            dst_ref=land.at[:, slot(q * pairs + pair)],
            send_sem=back_send.at[pair, step - 1],
            recv_sem=back_recv.at[pair, step - 1],
            device_id={"det": z * plane + other},
        )

    halves_of = [pl.ds(h * (rank // 2), rank // 2) for h in range(2)]

    def right_copy(pair, h):
        return pltpu.make_async_remote_copy(
            src_ref=from_left.at[pair, 1, halves_of[h], :],
            dst_ref=from_left.at[pair, 0, halves_of[h], :],
            send_sem=right_send.at[pair, h],
            recv_sem=right_recv.at[pair, h],
            device_id={"det": lax.rem(me + plane, plane * planes)},
        )

    def left_copy(pair, h):
        return pltpu.make_async_remote_copy(
            src_ref=from_right.at[pair, 1, halves_of[h], :],
            dst_ref=from_right.at[pair, 0, halves_of[h], :],
            send_sem=left_send.at[pair, h],
            recv_sem=left_recv.at[pair, h],
            device_id={"det": lax.rem(me + plane * (planes - 1), plane * planes)},
        )

    shape = (dets, dets)
    diagonal = lax.broadcasted_iota(jnp.int32, shape, 0) == lax.broadcasted_iota(jnp.int32, shape, 1)
    gain = jnp.sum(jnp.where(diagonal, gain_ref[...], 0.0), axis=1, keepdims=True)
    scale = jnp.broadcast_to(1.0 / gain, (dets, side))

    def to_cube(row, carry):
        cube[spread(row), :] = x_ref[:, column(row)] * scale
        return carry

    lax.fori_loop(0, side, to_cube, 0, unroll=8)
    first_table = (t1[0], t1[1])
    group = 8

    def first_stage(at, carry):
        rows = [pl.ds(pl.multiple_of((at * group + d) * side, side), side) for d in range(group)]
        section = product(first_table, split(jnp.concatenate([cube[row, :] for row in rows], axis=1)))
        for d in range(group):
            cube[rows[d], :] = section[:, d * side:(d + 1) * side]
        return carry

    lax.fori_loop(0, dets // group, first_stage, 0)
    at_ends = (z == 0).astype(jnp.int32) + (z == planes - 1).astype(jnp.int32)
    pl.semaphore_wait(barrier, plane + 1 - at_ends)

    def send_raw(pair, carry):
        for owner in range(plane):
            k = owner * pairs + pair
            cal[:, column(2 * k)] = cube[spread(2 * k), :]
            cal[:, column(2 * k + 1)] = cube[spread(2 * k + 1), :]
        for step in range(1, plane):
            raw_copy(pair, step).start()
        slab[pair, own_rows(q), :] = cal[:, slot(q * pairs + pair)]
        return carry

    lax.fori_loop(0, lead, send_raw, 0)
    in_plane = pl.ds(pl.multiple_of(z * plane * dets, 8), plane * dets)
    weight = split(weight_ref[in_plane, :].T)
    pattern = split(pattern_ref[in_plane, :])

    def measure_modes(pair):
        for step in range(1, plane):
            raw_copy(pair, step).wait_recv()
        part[pair] = product(weight, split(slab[pair]))

    measure_modes(0)

    def middle(real, imag, slots):
        turned = []
        for r, m, k in zip(real, imag, slots):
            cos, sin = turn[0, pl.ds(k, 1), :], turn[1, pl.ds(k, 1), :]
            turned.append(jnp.concatenate([r * cos + m * sin, m * cos - r * sin], axis=1))
        freq = product(split(jnp.concatenate(turned, axis=0)), (t2[0], t2[1]))
        weighted = []
        for at, k in enumerate(slots):
            noise = fold[own_rows(k), :]
            weighted.append(freq[at * dets:(at + 1) * dets] * jnp.concatenate([noise, noise], axis=1))
        section = product(split(jnp.concatenate(weighted, axis=0)), (t3[0], t3[1]))
        result = []
        for at, k in enumerate(slots):
            cos, sin = turn[0, pl.ds(k, 1), :], turn[1, pl.ds(k, 1), :]
            r, m = section[at * dets:(at + 1) * dets, :side], section[at * dets:(at + 1) * dets, side:]
            result.append((r * cos - m * sin, m * cos + r * sin))
        return result

    def one_step(i, carry):
        c_right = i - z
        c_left = i - (planes - 1 - z)
        for h in range(2):
            rows = halves_of[h]

            @pl.when((c_right >= 0) & (c_right < pairs))
            def _():
                @pl.when(z == 0)
                def _():
                    from_left[c_right, 1, rows, :] = part[c_right, rows, :]

                @pl.when(z > 0)
                def _():
                    right_copy(c_right, h).wait_recv()
                    from_left[c_right, 1, rows, :] = part[c_right, rows, :] + from_left[c_right, 0, rows, :]

                @pl.when(z < planes - 1)
                def _():
                    right_copy(c_right, h).start()

            @pl.when((c_left >= 0) & (c_left < pairs))
            def _():
                @pl.when(z == planes - 1)
                def _():
                    from_right[c_left, 1, rows, :] = part[c_left, rows, :]

                @pl.when(z < planes - 1)
                def _():
                    left_copy(c_left, h).wait_recv()
                    from_right[c_left, 1, rows, :] = part[c_left, rows, :] + from_right[c_left, 0, rows, :]

                @pl.when(z > 0)
                def _():
                    left_copy(c_left, h).start()

        @pl.when(i + lead < pairs)
        def _():
            send_raw(i + lead, 0)

        c = i - lag

        @pl.when((c >= 0) & (c < pairs))
        def _():
            coeff = from_left[c, 1] + (from_right[c, 1] - part[c])
            slab[c] = slab[c] - product(pattern, split(coeff))
            for step in range(1, plane):
                back_copy(c, step).start()
            land[:, slot(q * pairs + c)] = slab[c, own_rows(q), :]

        @pl.when(i + 1 < pairs)
        def _():
            measure_modes(i + 1)

        @pl.when(i == 0)
        def _():
            noise_copy.wait()

        @pl.when(i < 2)
        def _():
            def regroup(at, carry):
                row = i * (side // 2) + at
                out_ref[spread(row), :] = noise_ref[:, column(row)]
                return carry

            lax.fori_loop(0, side // 2, regroup, 0, unroll=4)

        @pl.when((i >= 2) & (i < 6))
        def _():
            def swap(at, carry):
                det = (i - 2) * (dets // 4) + at
                fold[pl.ds(det, side, stride=dets), :] = out_ref[column(det), :].T
                return carry

            lax.fori_loop(0, dets // 4, swap, 0, unroll=2)

        def add_mirror(at, carry):
            ks = [1 + at * 3 + j for j in range(3)]
            high, low = split(jnp.concatenate([fold[own_rows(side - k), :] for k in ks], axis=0))
            dot = functools.partial(jnp.dot, preferred_element_type=jnp.float32)
            mirror = dot(high, flip[...]) + dot(low, flip[...])
            for j, k in enumerate(ks):
                fold[own_rows(k), :] += mirror[j * dets:(j + 1) * dets]
            return carry

        triples = (side // 2 - 1) // 3

        @pl.when(i == 6)
        def _():
            lax.fori_loop(0, triples // 2, add_mirror, 0)

        @pl.when(i == 7)
        def _():
            lax.fori_loop(triples // 2, triples, add_mirror, 0)

        def transform(pair, carry):
            for step in range(1, plane):
                back_copy(pair, step).wait_recv()
            slots = [owner * pairs + pair for owner in range(plane)]
            real = [land[:, column(2 * k)] for k in slots]
            imag = [land[:, column(2 * k + 1)] for k in slots]
            for k, (r, m) in zip(slots, middle(real, imag, slots)):
                out_ref[spread(2 * k), :] = r
                out_ref[spread(2 * k + 1), :] = m

            @pl.when(pair == 0)
            def _():
                none = jnp.zeros((dets, side), jnp.float32)
                ends = middle([real[0], imag[0]], [none, none], [0, side // 2])
                out_ref[spread(0), :] = ends[0][0]
                out_ref[spread(1), :] = ends[1][0]
            return carry

        @pl.when((i >= max(mid_lag, ready + (ready - mid_lag) * (mid_lag < ready))) & (i < pairs + mid_lag))
        def _():
            transform(i - mid_lag, 0)

        if mid_lag < ready:
            @pl.when((i >= ready) & (i < ready + ready // 2))
            def _():
                lax.fori_loop(2 * (i - ready), 2 * (i - ready) + 2, transform, 0)

        return carry

    lax.fori_loop(0, pairs + mid_lag, one_step, 0)

    def finish(pair, carry):
        for step in range(1, plane):
            back_copy(pair, step).wait_send()
            raw_copy(pair, step).wait_send()

        @pl.when(z < planes - 1)
        def _():
            for h in range(2):
                right_copy(pair, h).wait_send()

        @pl.when(z > 0)
        def _():
            for h in range(2):
                left_copy(pair, h).wait_send()

        return carry

    lax.fori_loop(0, pairs, finish, 0)


def correct(stream, gains, noise, mode_pattern, mode_weights, tables, size):
    dets, samples = stream.shape
    rank = mode_pattern.shape[1]
    side = math.isqrt(samples)
    plane = 4 if size % 4 == 0 else 1
    planes = size // plane
    pairs = side // plane // 2
    rows = plane * dets
    f32 = jnp.float32
    vmem = pl.BlockSpec(memory_space=pltpu.VMEM)
    sem = pltpu.SemaphoreType.DMA
    coeffs = pltpu.VMEM((pairs, rank, 2 * side), f32)
    chain = pltpu.VMEM((pairs, 2, rank, 2 * side), f32)
    whole = pltpu.VMEM((dets, samples), f32)
    cube = pltpu.VMEM((dets * side, side), f32)
    return pl.pallas_call(
        functools.partial(correct_kernel, plane, planes),
        out_shape=jax.ShapeDtypeStruct((dets * side, side), f32),
        in_specs=[vmem, vmem, pl.BlockSpec(memory_space=pl.ANY)] + [vmem] * (2 + len(tables)),
        out_specs=pl.BlockSpec(memory_space=pltpu.VMEM),
        scratch_shapes=[
            whole, sem(()), cube, whole, pltpu.VMEM((pairs, rows, 2 * side), f32), coeffs, chain, chain, whole, cube,
            sem((pairs, plane)), sem((pairs, plane)), sem((pairs, 2)), sem((pairs, 2)),
            sem((pairs, 2)), sem((pairs, 2)), sem((pairs, plane)), sem((pairs, plane)),
        ],
        compiler_params=pltpu.CompilerParams(
            collective_id=0, has_side_effects=True, vmem_limit_bytes=60 * MIB
        ),
        name="correct",
    )(stream, gains, noise, mode_weights, mode_pattern, *tables)


def bin_kernel(x_ref, id_ref, hit_ref, sky_ref, t4, out_ref, acc_ref, count_ref, rows_ref, hits_ref):
    batch, side, _ = x_ref.shape
    per_row = PIX // side
    tiles = side // per_row
    packed = jnp.concatenate([x_ref[b] for b in range(batch)], axis=1)
    result = product((t4[0], t4[1]), split(packed))
    tiled = []
    for b in range(batch):
        part = result[:, b * side:(b + 1) * side]
        rows_ref[pl.ds(b * side, side), :] = part
        tiled.append(jnp.concatenate([part[p * tiles:(p + 1) * tiles] for p in range(per_row)], axis=1))
    for tile in range(tiles):
        for p in range(per_row):
            at = (tile * per_row + p) * side
            out_ref[:, at:at + side] = rows_ref[pl.ds(p * tiles + tile, batch, stride=side), :]
    high, low = split(jnp.concatenate(tiled, axis=0))
    blocks = acc_ref.shape[0]
    ladder = lax.broadcasted_iota(jnp.int32, (blocks, batch * tiles), 0)
    ids = jnp.concatenate([id_ref[b:b + 1, :] for b in range(batch)], axis=1)
    hits = jnp.concatenate([hit_ref[b:b + 1, :] for b in range(batch)], axis=1).astype(jnp.float32)
    table = jnp.where(ids == ladder, hits, 0.0)
    counts = table[:, :LANES]
    for at in range(LANES, batch * tiles, LANES):
        counts = counts + table[:, at:at + LANES]
    table = table.astype(jnp.bfloat16)
    dot = functools.partial(jnp.dot, preferred_element_type=jnp.float32)

    @pl.when(pl.program_id(0) == 0)
    def _():
        acc_ref[...] = jnp.zeros_like(acc_ref)
        hits_ref[...] = jnp.zeros_like(hits_ref)

    acc_ref[...] += dot(table, high) + dot(table, low)
    hits_ref[...] += counts

    @pl.when(pl.program_id(0) == pl.num_programs(0) - 1)
    def _():
        ladder = lax.broadcasted_iota(jnp.int32, (blocks, blocks), 0)
        place = jnp.where(sky_ref[...] == ladder, 1.0, 0.0).astype(jnp.bfloat16)
        total = acc_ref[...]
        high, low = split(total)
        rest = (total - high.astype(jnp.float32) - low.astype(jnp.float32)).astype(jnp.bfloat16)
        acc_ref[...] = dot(place, high) + (dot(place, low) + dot(place, rest))
        high, low = split(hits_ref[...])
        tally = split(dot(place, high) + dot(place, low))
        ones = jnp.ones((8, LANES), jnp.bfloat16)
        across = functools.partial(
            lax.dot_general, dimension_numbers=(((1,), (1,)), ((), ())), preferred_element_type=jnp.float32
        )
        count_ref[...] = (across(ones, tally[0]) + across(ones, tally[1]))[:1]


def finish_and_bin(packed, ids, hits, sky_rows, table):
    dets, side, _ = packed.shape
    batch = 16 if dets % 16 == 0 else 8
    tiles = side * side // PIX
    blocks = sky_rows.shape[1]
    line = pl.BlockSpec((batch, tiles), lambda i: (i, 0))
    return pl.pallas_call(
        bin_kernel,
        grid=(dets // batch,),
        out_shape=(
            jax.ShapeDtypeStruct((dets, side * side), jnp.float32),
            jax.ShapeDtypeStruct((blocks, PIX), jnp.float32),
            jax.ShapeDtypeStruct((1, blocks), jnp.float32),
        ),
        in_specs=[
            pl.BlockSpec((batch, side, side), lambda i: (i, 0, 0)),
            line,
            line,
            pl.BlockSpec((1, blocks), lambda i: (0, 0)),
            pl.BlockSpec(table.shape, lambda i: (0, 0, 0)),
        ],
        out_specs=(
            pl.BlockSpec((batch, side * side), lambda i: (i, 0)),
            pl.BlockSpec((blocks, PIX), lambda i: (0, 0)),
            pl.BlockSpec((1, blocks), lambda i: (0, 0)),
        ),
        scratch_shapes=[pltpu.VMEM((batch * side, side), jnp.float32), pltpu.VMEM((blocks, LANES), jnp.float32)],
        compiler_params=pltpu.CompilerParams(vmem_limit_bytes=60 * MIB),
        name="finish_and_bin",
    )(packed, ids, hits, sky_rows, table)


def map_kernel(
    plane, planes, acc_ref, count_ref, out_ref,
    near, near_tally, partial, tally, far, far_tally,
    near_send, near_recv, near_tally_send, near_tally_recv, far_send, far_recv, far_tally_send, far_tally_recv,
):
    me = lax.axis_index("det")
    z, q = me // plane, me % plane
    rows, columns = out_ref.shape
    barrier = pltpu.get_barrier_semaphore()

    def neighbour(step):
        return z * plane + lax.rem(q + step, plane)

    def beyond(step):
        return lax.rem(me + step * plane, plane * planes)

    for step in range(1, plane):
        pl.semaphore_signal(barrier, inc=1, device_id={"det": neighbour(step)})
    for step in range(1, planes):
        pl.semaphore_signal(barrier, inc=1, device_id={"det": beyond(step)})
    pl.semaphore_wait(barrier, plane + planes - 2)

    def share(owner):
        return pl.ds(pl.multiple_of(owner * rows, 8), rows)

    def remote(source, target, send_sem, recv_sem, device):
        return pltpu.make_async_remote_copy(
            src_ref=source, dst_ref=target, send_sem=send_sem, recv_sem=recv_sem, device_id={"det": device}
        )

    first, second = [], []
    for step in range(1, plane):
        source = acc_ref.at[:, share(lax.rem(q + step, plane)), :]
        at = step - 1
        first.append((
            remote(source, near.at[at], near_send.at[at], near_recv.at[at], neighbour(step)),
            remote(count_ref, near_tally.at[at], near_tally_send.at[at], near_tally_recv.at[at], neighbour(step)),
        ))
    for step in range(1, planes):
        at = step - 1
        source = partial.at[lax.rem(z + step, planes)]
        second.append((
            remote(source, far.at[at], far_send.at[at], far_recv.at[at], beyond(step)),
            remote(tally, far_tally.at[at], far_tally_send.at[at], far_tally_recv.at[at], beyond(step)),
        ))
    for pair in first:
        for copy in pair:
            copy.start()
    sums, counts = acc_ref[:, share(q), :], count_ref[...]
    for at, pair in enumerate(first):
        for copy in pair:
            copy.wait_recv()
        sums, counts = sums + near[at], counts + near_tally[at]
    partial[...] = sums
    tally[...] = counts
    for pair in second:
        for copy in pair:
            copy.start()
    sums = partial[z]
    for at, pair in enumerate(second):
        for copy in pair:
            copy.wait_recv()
        sums, counts = sums + far[at], counts + far_tally[at]
    shape = (rows, counts.shape[1])
    mine = lax.broadcasted_iota(jnp.int32, shape, 1) == lax.broadcasted_iota(jnp.int32, shape, 0) + me * rows
    counts = jnp.sum(jnp.where(mine, counts, 0.0), axis=1, keepdims=True)
    out_ref[...] = sums / jnp.sqrt(1.0 + counts)
    for pair in first + second:
        for copy in pair:
            copy.wait_send()


def combine_map(acc, counts, size):
    blocks, columns = acc.shape
    rows = blocks // size
    plane = 4 if size % 4 == 0 else 1
    planes = size // plane
    near, far = max(1, plane - 1), max(1, planes - 1)
    sems = [pltpu.SemaphoreType.DMA((near,))] * 4 + [pltpu.SemaphoreType.DMA((far,))] * 4
    f32 = jnp.float32
    return pl.pallas_call(
        functools.partial(map_kernel, plane, planes),
        out_shape=jax.ShapeDtypeStruct((rows, columns), f32),
        in_specs=[pl.BlockSpec(memory_space=pltpu.VMEM)] * 2,
        out_specs=pl.BlockSpec(memory_space=pltpu.VMEM),
        scratch_shapes=[
            pltpu.VMEM((near, planes, rows, columns), f32),
            pltpu.VMEM((near, 1, blocks), f32),
            pltpu.VMEM((planes, rows, columns), f32),
            pltpu.VMEM((1, blocks), f32),
            pltpu.VMEM((far, rows, columns), f32),
            pltpu.VMEM((far, 1, blocks), f32),
            *sems,
        ],
        compiler_params=pltpu.CompilerParams(collective_id=1, has_side_effects=True),
        name="combine_map",
    )(acc.reshape(planes, plane * rows, columns), counts)


def shards(size, timestream, gains, mode_pattern, mode_weights, noise_weight, block_ids, hits, sky_rows):
    items, dets, samples = timestream.shape
    side = math.isqrt(samples)
    *tables, last = [jnp.asarray(table) for table in transform_tables(side)]
    packed = correct(
        timestream.reshape(items * dets, samples), gains, noise_weight, mode_pattern, mode_weights,
        tables, size,
    )
    filtered, acc, counts = finish_and_bin(
        packed.reshape(dets, side, side), block_ids.reshape(dets, -1), hits.reshape(dets, -1), sky_rows[None, :], last
    )
    return (filtered.reshape(items, dets, samples), combine_map(acc, counts, size))


def solution(mesh):
    in_specs = (
        P("grp", "det", None),
        P("grp", "det"),
        P("grp", None),
        P("grp", None),
        P(("grp", "det"), None),
        P("grp", "det", None),
        P("grp", "det", None),
        P("grp"),
    )
    out_specs = (P("grp", "det", None), P(("grp", "det"), None))
    body = functools.partial(shards, mesh.shape["det"])
    return jax.shard_map(body, mesh=mesh, in_specs=in_specs, out_specs=out_specs, check_vma=False)
```
